512 devices in a mesh: ctx: 64 (over y, z_lo, core), head: 8 (over z_hi, x).
Axes of the slice: x: 4, y: 4, z: 16 (z_hi: 2, z_lo: 8; z = z_hi * 8 + z_lo), core: 2. Of those that a mesh axis runs over, the one named last changes fastest.
Arguments:
- hidden: bfloat16 [4096, 7168], P('ctx', 'head'), may hold values from -6 to 6
- latent_proj: bfloat16 [7168, 576], P('head'), may hold values from -0.0625 to 0.0625
- norm_gain: float32 [512], replicated, may hold values from 0.1 to 1.9
- queries: bfloat16 [4096, 64, 192], P('ctx', 'head'), may hold values from -110 to 110
- key_absorb: bfloat16 [64, 128, 512], P('head'), may hold values from -0.5 to 0.5
- value_absorb: bfloat16 [64, 512, 128], P('head'), may hold values from -0.25 to 0.25
- pool_blocks: bfloat16 [256, 128, 576], P('ctx'), may hold values from -6 to 6
- hit_block: int32 [2], replicated, may hold values from 0 to 255, as said below
Outputs:
- mixed: bfloat16 [4096, 64, 128], P('ctx', 'head')
The draws below stay inside these ranges and needn't reach their ends.
Inputs may be any that keep to these rules, and one draw needn't show every extreme that they name: `hit_block`: 2 different pool blocks, one of them the pool's last block.
All inputs are finite; a program needn't handle non-finite values.
Results may differ from the reference program's by a relative error of at most 0.017.
The reference program's roundings to bfloat16 on the way (of `new_keys`, `absorbed`, `query_full`, `keys` and `attended`) count: a program that leaves them out, or rounds other values in their place, can miss the bound.
Values may be sent and summed in bfloat16 or wider, within the bound.
No kernel may reach another device: no remote copies, remote signals or barrier semaphores. Data moves between devices by JAX's collectives and lax.ppermute only.
A program may use at most 64 MiB of HBM per device.

```python
import math
import jax
import jax.numpy as jnp
from jax import lax

D = 7168
KV_RANK = 512
ROPE = 64
NOPE = 128
V_HEAD = 128
HEADS = 64
BLOCK = 128
TOK_DEV = 64
NHIT = 2
TOKENS = 4096
POOL = 256


def draw_queries(key, part):
    key = jax.random.fold_in(key, 11)
    shape = (TOKENS, HEADS, NOPE + ROPE)
    values = jnp.clip(jax.random.normal(key, shape, jnp.float32), -4.0, 4.0)
    return values.astype(jnp.bfloat16)


def draw_hit_block(key, part):
    key = jax.random.fold_in(key, 5)
    others = jax.random.permutation(key, POOL - 1)[:NHIT - 1].astype(jnp.int32)
    chosen = jnp.concatenate([others, jnp.full((1,), POOL - 1, jnp.int32)])
    return jax.random.permutation(jax.random.fold_in(key, 1), chosen).astype(jnp.int32)


def levels(rng, shape, split, low, largest):
    level, own = 1.0, jax.random.fold_in(rng, 6)
    for dim, parts in split:
        heights = jnp.exp(jax.random.uniform(jax.random.fold_in(own, dim), (parts,), jnp.float32, low / len(split), largest / len(split)))
        level = level * jnp.repeat(heights, shape[dim] // parts).reshape([-1 if axis == dim else 1 for axis in range(len(shape))])
    return level


def gaussian(key, shape, deviation, limit, split=(), kind=jnp.bfloat16):
    entries = deviation * jax.random.normal(key, shape, jnp.float32)
    if split:
        entries = entries * levels(key, shape, split, -0.22, 0.18)
    return jnp.clip(entries, -limit, limit).astype(kind)


def setup_inputs(seed: int = 0) -> dict:
    key_of = jax.random.split(jax.random.key(seed), 9)
    hidden = gaussian(key_of[0], (TOKENS, D), 1.0, 6.0, ((0, 64), (1, 8)))
    latent_proj = gaussian(key_of[1], (D, KV_RANK + ROPE), D ** -0.5, 0.0625, ((0, 8),))
    norm_gain = jnp.clip(1.0 + 0.18 * jax.random.normal(key_of[2], (KV_RANK,), jnp.float32), 0.1, 1.9)
    queries = draw_queries(jax.random.fold_in(key_of[8], 71), 0)
    key_absorb = gaussian(key_of[4], (HEADS, NOPE, KV_RANK), NOPE ** -0.5, 0.5, ((0, 8),))
    value_absorb = gaussian(key_of[5], (HEADS, KV_RANK, V_HEAD), KV_RANK ** -0.5, 0.25, ((0, 8),))
    pool_blocks = gaussian(key_of[6], (POOL, BLOCK, KV_RANK + ROPE), 1.0, 6.0, ((0, 64),))
    hit_block = draw_hit_block(jax.random.fold_in(key_of[8], 71), 0)
    return dict(hidden=hidden, latent_proj=latent_proj, norm_gain=norm_gain, queries=queries, key_absorb=key_absorb, value_absorb=value_absorb, pool_blocks=pool_blocks, hit_block=hit_block)


EPS = 1e-06
BIG = -1e+30

def rotate(vector, angle):
    half = vector.shape[-1] // 2
    first = vector[..., :half]
    second = vector[..., half:]
    cosine = jnp.cos(angle)
    sine = jnp.sin(angle)
    return jnp.concatenate([first * cosine - second * sine, second * cosine + first * sine], axis=-1)

def angles_for(positions, width):
    half = width // 2
    inverse = 10000.0 ** (-jnp.arange(half, dtype=jnp.float32) / half)
    return positions[:, None] * inverse[None, :]

def finish(raw, positions, norm_gain, rank):
    latent = raw[:, :rank]
    scaled = latent * lax.rsqrt(lax.optimization_barrier(jnp.mean(latent * latent, axis=1, keepdims=True)) + EPS) * norm_gain[None, :]
    rotated = rotate(raw[:, rank:], angles_for(positions, raw.shape[1] - rank))
    return jnp.concatenate([scaled, rotated], axis=1).astype(jnp.bfloat16)

def reference(hidden, latent_proj, norm_gain, queries, key_absorb, value_absorb, pool_blocks, hit_block):
    prefix_len = NHIT * BLOCK
    raw = jnp.dot(hidden, latent_proj, preferred_element_type=jnp.float32)
    positions = (prefix_len + jnp.arange(TOKENS)).astype(jnp.float32)
    new_keys = finish(raw, positions, norm_gain, KV_RANK)
    prefix = pool_blocks[hit_block].reshape(prefix_len, KV_RANK + ROPE)
    keys = jnp.concatenate([prefix, new_keys], axis=0)
    absorbed = jnp.einsum('thn,hnc->thc', queries[:, :, :NOPE].astype(jnp.float32), key_absorb.astype(jnp.float32)).astype(jnp.bfloat16)
    rotated_q = rotate(queries[:, :, NOPE:].astype(jnp.float32), angles_for(positions, ROPE)[:, None, :]).astype(jnp.bfloat16)
    query_full = jnp.concatenate([absorbed, rotated_q], axis=2)
    keys_wide = keys.astype(jnp.float32)
    values_wide = keys_wide[:, :KV_RANK]
    key_index = (jnp.arange(prefix_len + TOKENS) - prefix_len).astype(jnp.int32)
    scale = 1.0 / math.sqrt(NOPE + ROPE)

    def one_block(index):
        start = (index * TOK_DEV).astype(jnp.int32)
        block_q = lax.dynamic_slice_in_dim(query_full, start, TOK_DEV, 0).astype(jnp.float32)
        scores = jnp.einsum('thc,kc->thk', block_q, keys_wide) * scale
        token_index = (start + jnp.arange(TOK_DEV)).astype(jnp.int32)
        visible = key_index[None, None, :] <= token_index[:, None, None]
        scores = jnp.where(visible, scores, BIG)
        peak = lax.optimization_barrier(jnp.max(scores, axis=2, keepdims=True))
        weights = jnp.where(visible, jnp.exp(scores - peak), 0.0)
        total = lax.optimization_barrier(jnp.sum(weights, axis=2))
        rounded = lax.optimization_barrier(weights.astype(jnp.bfloat16)).astype(jnp.float32)
        summed = jnp.einsum('thk,kc->thc', rounded, values_wide)
        return (summed / total[..., None]).astype(jnp.bfloat16)
    attended = lax.map(one_block, jnp.arange(TOKENS // TOK_DEV, dtype=jnp.int32))
    attended = attended.reshape(TOKENS, HEADS, KV_RANK)
    mixed = jnp.einsum('thc,hcv->thv', attended.astype(jnp.float32), value_absorb.astype(jnp.float32))
    return mixed.astype(jnp.bfloat16)
```

```python
import functools
import math

import jax
import jax.numpy as jnp
from jax import lax
from jax.experimental import pallas as pl
from jax.experimental.pallas import tpu as pltpu
from jax.sharding import Mesh, PartitionSpec as P

EPS = 1e-06
NEG = -1e30
BF = jnp.bfloat16
F32 = jnp.float32

NY, NZ, NC, NH, NX = 4, 8, 2, 2, 4
CTX = ("y", "zl", "c")
HEAD = ("zh", "x")

TOK = 64
RANK = 512
WIDTH = 576
NOPE = 128
ROPE = 64
QW = 192
HEADS = 8
BLOCK = 128
POOL_HERE = 4
HITS = 2
XROWS = TOK // NX
PREV = 8
PIECE = HITS * PREV
QROWS = TOK * HEADS
PAY = 3 * PIECE
CHUNK = NZ * XROWS + PIECE
NEW = NC * NX * NZ * XROWS
PRE = NX * PIECE
KEYS = NEW + PRE
STAT = 32
OUTR = QROWS + STAT

VMEM = pl.BlockSpec(memory_space=pltpu.VMEM)
SMEM = pl.BlockSpec(memory_space=pltpu.SMEM)


def params(mib=32):
    return pltpu.CompilerParams(vmem_limit_bytes=mib * 2**20)


def swap_halves(v):
    half = v.shape[-1] // 2
    return jnp.concatenate([v[:, half:], v[:, :half]], axis=1)


def prepare_kernel(ids, q_ref, cos_ref, sin_ref, pool_ref, own_q, own_p, p1, p2, p3, qn, qr, pre):
    y, x = ids[0], ids[1]
    flat = q_ref[...].astype(F32).reshape(QROWS, QW)
    qn[...] = flat[:, :NOPE]
    qr[:, :ROPE] = flat[:, NOPE:]
    cosine = cos_ref[...]
    sine = sin_ref[...]
    for h in range(HEADS):
        rope = qr[pl.ds(h, TOK, stride=HEADS), :][:, :ROPE]
        rope = rope * cosine + swap_halves(rope) * sine
        out = jnp.concatenate([qn[pl.ds(h, TOK, stride=HEADS), :], rope], axis=1).astype(BF)
        own_q[h * TOK : (h + 1) * TOK, :] = out
        for p in (p1, p2, p3):
            p[PAY + h * TOK : PAY + (h + 1) * TOK, :] = out
    start = pl.multiple_of(x * 32, 32)
    for b in range(HITS):
        pre[b * 32 : (b + 1) * 32, :] = pool_ref[ids[8 + b], pl.ds(start, 32), :].astype(F32)
    for shift, p in enumerate((own_p, p1, p2, p3)):
        target = lax.rem(y - shift + NY, NY)
        piece = jnp.concatenate(
            [pre[pl.ds(pl.multiple_of(b * 32 + target * PREV, PREV), PREV), :] for b in range(HITS)],
            axis=0,
        )
        for s in range(3):
            p[s * PIECE : (s + 1) * PIECE, :] = piece[:, s * QW : (s + 1) * QW].astype(BF)


def norm_kernel(ids, s_ref, r_ref, gain_ref, cos_ref, sin_ref, own_p, p1, p2, p3, out):
    y, x = ids[0], ids[1]
    raw = s_ref[...] + r_ref[...]
    latent = raw[:, :RANK]
    mean = jnp.mean(latent * latent, axis=1, keepdims=True)
    scaled = latent * lax.rsqrt(mean + EPS) * gain_ref[...]
    start = pl.multiple_of(x * XROWS, XROWS)
    cosine = cos_ref[pl.ds(start, XROWS), :]
    sine = sin_ref[pl.ds(start, XROWS), :]
    rope = raw[:, RANK:]
    rope = rope * cosine + swap_halves(rope) * sine
    keys = jnp.concatenate([scaled, rope], axis=1).astype(BF)
    pieces = []
    row = lax.broadcasted_iota(jnp.int32, (PIECE, QW), 0)
    for s in range(3):
        cand = [p[s * PIECE : (s + 1) * PIECE, :].astype(F32) for p in (own_p, p1, p2, p3)]
        halves = []
        for b in range(HITS):
            shift = lax.rem(ids[2 + b] - y + NY, NY)
            halves.append(
                jnp.where(
                    shift == 0,
                    cand[0],
                    jnp.where(shift == 1, cand[1], jnp.where(shift == 2, cand[2], cand[3])),
                )
            )
        pieces.append(jnp.where(row < PREV, halves[0], halves[1]))
    piece = jnp.concatenate(pieces, axis=1).astype(BF)
    for k in range(NZ):
        out[k, 0:XROWS, :] = keys
        out[k, XROWS : XROWS + PIECE, :] = piece


def pick(first, second):
    row = lax.broadcasted_iota(jnp.int32, (PIECE, WIDTH), 0)
    return jnp.where(row < PREV, first.astype(F32), second.astype(F32)).astype(BF)


def pack_kernel(ids, z_ref, out):
    piece = pick(z_ref[ids[4], XROWS:, :], z_ref[ids[5], XROWS:, :])
    for k in range(NX):
        for z in range(NZ):
            out[k, z * XROWS : (z + 1) * XROWS, :] = z_ref[z, 0:XROWS, :]
        out[k, NZ * XROWS :, :] = piece


def column_to_row(col):
    eye = lax.broadcasted_iota(jnp.int32, (128, 128), 0) == lax.broadcasted_iota(
        jnp.int32, (128, 128), 1
    )
    rows = [
        jnp.sum(jnp.where(eye, col[i * 128 : (i + 1) * 128, :], 0.0), axis=0, keepdims=True)
        for i in range(col.shape[0] // 128)
    ]
    return jnp.concatenate(rows, axis=0)


def row_to_column(rows):
    eye = lax.broadcasted_iota(jnp.int32, (128, 128), 0) == lax.broadcasted_iota(
        jnp.int32, (128, 128), 1
    )
    cols = [
        jnp.sum(jnp.where(eye, rows[i : i + 1, :], 0.0), axis=1, keepdims=True)
        for i in range(rows.shape[0])
    ]
    return jnp.concatenate(cols, axis=0)


def three(v):
    high = v.astype(BF).astype(F32)
    mid = (v - high).astype(BF).astype(F32)
    low = v - high - mid
    return [high, mid, low]


def attend_kernel(ids, q0, q1, q2, q3, here, there, wk, wv, out, keys, qfull, att):
    y = ids[0]
    zl = ids[6]
    c = ids[7]
    scale = 1.0 / math.sqrt(QW)
    for i, ref in enumerate((here, there)):
        for j in range(NX):
            n = (i * NX + j) * NZ * XROWS
            keys[n : n + NZ * XROWS, :] = ref[j, 0 : NZ * XROWS, :]
    for j in range(NX):
        mine = here[j, NZ * XROWS :, :].astype(F32)
        other = there[j, NZ * XROWS :, :].astype(F32)
        keys[NEW + j * PIECE : NEW + (j + 1) * PIECE, :] = pick(
            jnp.where(ids[10] == c, mine, other), jnp.where(ids[11] == c, mine, other)
        )
    sources = (q0, q1, q2, q3)
    starts = (0, PAY, PAY, PAY)
    for h in range(HEADS):
        rows = jnp.concatenate(
            [q[s + h * TOK : s + (h + 1) * TOK, :] for q, s in zip(sources, starts)], axis=0
        )
        absorbed = jnp.dot(rows[:, :NOPE], wk[h], preferred_element_type=F32).astype(BF)
        full = jnp.concatenate([absorbed, rows[:, NOPE:]], axis=1)
        for g in range(NY):
            qfull[g, h * TOK : (h + 1) * TOK, :] = full[g * TOK : (g + 1) * TOK, :]

    col = lax.broadcasted_iota(jnp.int32, (1, KEYS), 1)
    zz = lax.rem(lax.div(col, XROWS), NZ)
    xx = lax.rem(lax.div(col, XROWS * NZ), NX)
    cc = lax.div(col, XROWS * NZ * NX)
    cc = jnp.where(cc == 0, c, 1 - c)
    token = zz * (NC * TOK) + cc * TOK + xx * XROWS + lax.rem(col, XROWS) + y * (NZ * NC * TOK)
    token = jnp.where(col < NEW, token, -1)
    for g in range(NY):
        yq = lax.rem(y + g, NY)
        scores = lax.dot_general(
            qfull[g], keys[...], (((1,), (1,)), ((), ())), preferred_element_type=F32
        )
        mine = lax.rem(lax.broadcasted_iota(jnp.int32, (QROWS, 1), 0), TOK)
        mine = mine + (yq * NZ * NC + zl * NC + c) * TOK
        visible = token <= mine
        scores = jnp.where(visible, scores, NEG)
        peak = jnp.max(scores, axis=1, keepdims=True)
        weights = jnp.exp((scores - peak) * scale)
        total = jnp.sum(weights, axis=1, keepdims=True)
        accum = jnp.dot(weights.astype(BF), keys[:, :RANK], preferred_element_type=F32)
        partial = (accum / total).astype(BF)
        for h in range(HEADS):
            att[h, g * TOK : (g + 1) * TOK, :] = partial[h * TOK : (h + 1) * TOK, :]
        stats = [column_to_row(v) for v in three(peak * scale) + three(total)]
        stats.append(jnp.zeros((STAT - 4 * len(stats), 128), F32))
        out[yq, QROWS:, :] = jnp.concatenate(stats, axis=0).astype(BF)
    for h in range(HEADS):
        mixed = jnp.dot(att[h], wv[h], preferred_element_type=F32).astype(BF)
        for g in range(NY):
            yq = lax.rem(y + g, NY)
            out[yq, h * TOK : (h + 1) * TOK, :] = mixed[g * TOK : (g + 1) * TOK, :]


def merge_kernel(p_ref, out, flat):
    peaks, totals = [], []
    for s in range(NY):
        stats = p_ref[s, QROWS:, :].astype(F32)
        peaks.append(row_to_column(stats[0:4] + stats[4:8] + stats[8:12]))
        totals.append(row_to_column(stats[12:16] + stats[16:20] + stats[20:24]))
    peak = functools.reduce(jnp.maximum, peaks)
    weights = [t * jnp.exp(p - peak) for t, p in zip(totals, peaks)]
    total = functools.reduce(jnp.add, weights)
    mixed = sum(p_ref[s, 0:QROWS, :].astype(F32) * (weights[s] / total) for s in range(NY))
    for h in range(HEADS):
        flat[pl.ds(h, TOK, stride=HEADS), :] = mixed[h * TOK : (h + 1) * TOK, :]
    out[...] = flat[...].reshape(TOK, HEADS, 128).astype(BF)


def on_device(
    hidden, latent_proj, norm_gain, queries, key_absorb, value_absorb, pool_blocks, hit_block
):
    y, zl, c, x = (lax.axis_index(a) for a in ("y", "zl", "c", "x"))
    owner = hit_block // POOL_HERE
    ids = jnp.concatenate(
        [
            jnp.stack([y, x]),
            owner // (NZ * NC),
            (owner // NC) % NZ,
            jnp.stack([zl, c]),
            hit_block % POOL_HERE,
            owner % NC,
        ]
    ).astype(jnp.int32)
    first = HITS * BLOCK + ((y * NZ + zl) * NC + c) * TOK
    positions = (first + jnp.arange(TOK)).astype(F32)
    half = ROPE // 2
    inverse = 10000.0 ** (-jnp.arange(half, dtype=F32) / half)
    angle = positions[:, None] * inverse[None, :]
    cosine, sine = jnp.cos(angle), jnp.sin(angle)
    cosine = jnp.concatenate([cosine, cosine], axis=1)
    sine = jnp.concatenate([-sine, sine], axis=1)

    pay = jax.ShapeDtypeStruct((PAY + QROWS, QW), BF)
    own_q, own_p, p1, p2, p3 = pl.pallas_call(
        prepare_kernel,
        out_shape=[
            jax.ShapeDtypeStruct((QROWS, QW), BF),
            jax.ShapeDtypeStruct((PAY, QW), BF),
            pay,
            pay,
            pay,
        ],
        in_specs=[SMEM] + [VMEM] * 4,
        out_specs=[VMEM] * 5,
        scratch_shapes=[
            pltpu.VMEM((QROWS, 128), F32),
            pltpu.VMEM((QROWS, 128), F32),
            pltpu.VMEM((HITS * 32, WIDTH), F32),
        ],
        compiler_params=params(),
        name="prepare",
    )(ids, queries, cosine, sine, pool_blocks)
    received = [
        lax.ppermute(p, "y", [(i, (i - k) % NY) for i in range(NY)])
        for k, p in zip((1, 2, 3), (p1, p2, p3))
    ]

    partial_raw = jnp.dot(hidden, latent_proj, preferred_element_type=F32)
    parts = lax.all_to_all(partial_raw.reshape(NX, XROWS, WIDTH), "x", 0, 0)
    mine = jnp.sum(parts, axis=0)
    other = lax.ppermute(mine, "zh", [(0, 1), (1, 0)])
    head = pl.BlockSpec((PAY, QW), lambda i: (0, 0))

    def whole(shape):
        return pl.BlockSpec(shape, lambda i: (0,) * len(shape))

    packed = pl.pallas_call(
        norm_kernel,
        grid=(1,),
        out_shape=jax.ShapeDtypeStruct((NZ, XROWS + PIECE, WIDTH), BF),
        in_specs=[
            SMEM,
            whole((XROWS, WIDTH)),
            whole((XROWS, WIDTH)),
            whole((1, RANK)),
            whole((TOK, ROPE)),
            whole((TOK, ROPE)),
            head,
            head,
            head,
            head,
        ],
        out_specs=whole((NZ, XROWS + PIECE, WIDTH)),
        compiler_params=params(),
        name="norm",
    )(ids, mine, other, norm_gain[None, :], cosine, sine, own_p, *received)
    along_z = lax.all_to_all(packed, "zl", 0, 0)
    packed = pl.pallas_call(
        pack_kernel,
        out_shape=jax.ShapeDtypeStruct((NX, CHUNK, WIDTH), BF),
        in_specs=[SMEM, VMEM],
        out_specs=VMEM,
        compiler_params=params(),
        name="pack",
    )(ids, along_z)
    along_x = lax.all_to_all(packed, "x", 0, 0)
    from_core = lax.ppermute(along_x, "c", [(0, 1), (1, 0)])
    out = pl.pallas_call(
        attend_kernel,
        out_shape=jax.ShapeDtypeStruct((NY, OUTR, 128), BF),
        in_specs=[SMEM] + [VMEM] * 8,
        out_specs=VMEM,
        scratch_shapes=[
            pltpu.VMEM((KEYS, WIDTH), BF),
            pltpu.VMEM((NY, QROWS, WIDTH), BF),
            pltpu.VMEM((HEADS, NY * TOK, RANK), BF),
        ],
        compiler_params=params(48),
        name="attend",
    )(ids, own_q, *received, along_x, from_core, key_absorb, value_absorb)
    back = lax.all_to_all(out, "y", 0, 0)
    return pl.pallas_call(
        merge_kernel,
        out_shape=jax.ShapeDtypeStruct((TOK, HEADS, 128), BF),
        in_specs=[VMEM],
        out_specs=VMEM,
        scratch_shapes=[pltpu.VMEM((QROWS, 128), F32)],
        compiler_params=params(),
        name="merge",
    )(back)


def solution(mesh):
    fine = Mesh(mesh.devices.reshape(NY, NZ, NC, NH, NX), CTX + HEAD)
    placed = (
        P(CTX, HEAD),
        P(HEAD, None),
        P(),
        P(CTX, HEAD, None),
        P(HEAD, None, None),
        P(HEAD, None, None),
        P(CTX, None, None),
        P(),
    )
    return jax.shard_map(
        on_device, mesh=fine, in_specs=placed, out_specs=P(CTX, HEAD, None), check_vma=False
    )
```

```python
import functools
import math

import jax
import jax.numpy as jnp
from jax import lax
from jax.experimental import pallas as pl
from jax.experimental.pallas import tpu as pltpu
from jax.sharding import Mesh, PartitionSpec as P

EPS = 1e-06
NEG = -1e30
BF = jnp.bfloat16
F32 = jnp.float32

NY, NZ, NC, NH, NX = 4, 8, 2, 2, 4
CTX = ("y", "zl", "c")
HEAD = ("zh", "x")

TOK = 64
RANK = 512
WIDTH = 576
NOPE = 128
ROPE = 64
QW = 192
HEADS = 8
BLOCK = 128
POOL_HERE = 4
HITS = 2
XROWS = TOK // NX
PREV = 8
PIECE = HITS * PREV
QROWS = TOK * HEADS
LANES = 128
BANDS = RANK // LANES
PAY = (BANDS + 1) * PIECE
PAYQ = PAY + QROWS
PAYR = PAYQ + QROWS // 2
RAWR = BANDS * XROWS + XROWS // 2
ZBAND = XROWS + PIECE
ZROWS = BANDS * ZBAND + 16
SPAN = NZ * XROWS
XBAND = SPAN + PIECE
XROPE = BANDS * XBAND
XPRE = XROPE + SPAN // 2
CHUNK = XPRE + PIECE
NEW = NC * NX * NZ * XROWS
PRE = NX * PIECE
KEYS = NEW + PRE
STAT = 32
OUTR = QROWS + STAT
ROWS = 512

VMEM = pl.BlockSpec(memory_space=pltpu.VMEM)
SMEM = pl.BlockSpec(memory_space=pltpu.SMEM)


def params(mib=32):
    return pltpu.CompilerParams(vmem_limit_bytes=mib * 2**20)


def swap_halves(v):
    half = v.shape[-1] // 2
    return jnp.concatenate([v[:, half:], v[:, :half]], axis=1)


def prepare_kernel(
    hit, q_ref, cos_ref, sin_ref, pool_ref, own_q, own_p, p1, p2, p3, qn, qr, found, pre, sem
):
    y, x = lax.axis_index("y"), lax.axis_index("x")
    copies = [
        pltpu.make_async_copy(pool_ref.at[lax.rem(hit[b], POOL_HERE)], found.at[b], sem.at[b])
        for b in range(HITS)
    ]
    for copy in copies:
        copy.start()
    flat = q_ref[...].astype(F32).reshape(QROWS, QW)
    qn[...] = flat[:, :NOPE]
    qr[:, :ROPE] = flat[:, NOPE:]
    cosine = cos_ref[...]
    sine = sin_ref[...]
    ropes = []
    for h in range(HEADS):
        rope = qr[pl.ds(h, TOK, stride=HEADS), :][:, :ROPE]
        ropes.append(rope * cosine + swap_halves(rope) * sine)
        out = qn[pl.ds(h, TOK, stride=HEADS), :].astype(BF)
        own_q[h * TOK : (h + 1) * TOK, :] = out
        for p in (p1, p2, p3):
            p[PAY + h * TOK : PAY + (h + 1) * TOK, :] = out
    for h in range(HEADS // 2):
        out = jnp.concatenate([ropes[h], ropes[h + HEADS // 2]], axis=1).astype(BF)
        own_q[QROWS + h * TOK : QROWS + (h + 1) * TOK, :] = out
        for p in (p1, p2, p3):
            p[PAYQ + h * TOK : PAYQ + (h + 1) * TOK, :] = out
    for b in range(HITS):
        copies[b].wait()
        pre[b * BLOCK : (b + 1) * BLOCK, :] = found[b].astype(F32).T
    for shift, p in enumerate((own_p, p1, p2, p3)):
        target = lax.rem(y - shift + NY, NY)
        first = x * (BLOCK // NX) + target * PREV
        piece = jnp.concatenate(
            [pre[pl.ds(pl.multiple_of(b * BLOCK + first, PREV), PREV), :] for b in range(HITS)],
            axis=0,
        )
        piece = jnp.concatenate([piece, piece[:, RANK:]], axis=1).astype(BF)
        for s in range(BANDS + 1):
            p[s * PIECE : (s + 1) * PIECE, :] = piece[:, s * LANES : (s + 1) * LANES]


def project_kernel(hidden, proj, out):
    partial = lax.dot_general(
        hidden[...], proj[...], (((1,), (1,)), ((), ())), preferred_element_type=F32
    )
    for k in range(NX):
        rows = partial[k * XROWS : (k + 1) * XROWS]
        for s in range(BANDS):
            out[k, s * XROWS : (s + 1) * XROWS, :] = rows[:, s * LANES : (s + 1) * LANES]
        rope = rows[:, RANK:]
        half = XROWS // 2
        out[k, BANDS * XROWS :, :] = jnp.concatenate([rope[:half], rope[half:]], axis=1)


def norm_kernel(ids, s_ref, r_ref, gain_ref, cos_ref, sin_ref, own_p, p1, p2, p3, out):
    y, x = ids[0], ids[1]
    raw = s_ref[...] + r_ref[...]
    latent = jnp.concatenate([raw[s * XROWS : (s + 1) * XROWS] for s in range(BANDS)], axis=1)
    rope = raw[BANDS * XROWS :]
    rope = jnp.concatenate([rope[:, :ROPE], rope[:, ROPE:]], axis=0)
    mean = jnp.mean(latent * latent, axis=1, keepdims=True)
    scaled = (latent * lax.rsqrt(mean + EPS) * gain_ref[...]).astype(BF)
    start = pl.multiple_of(x * XROWS, XROWS)
    cosine = cos_ref[pl.ds(start, XROWS), :]
    sine = sin_ref[pl.ds(start, XROWS), :]
    rope = rope * cosine + swap_halves(rope) * sine
    shifts = [lax.rem(ids[2 + b] - y + NY, NY) for b in range(HITS)]
    row = lax.broadcasted_iota(jnp.int32, (PIECE, LANES), 0)
    bands = []
    for s in range(BANDS + 1):
        cand = [p[s * PIECE : (s + 1) * PIECE, :].astype(F32) for p in (own_p, p1, p2, p3)]
        halves = [
            jnp.where(
                shift == 0,
                cand[0],
                jnp.where(shift == 1, cand[1], jnp.where(shift == 2, cand[2], cand[3])),
            )
            for shift in shifts
        ]
        bands.append(jnp.where(row < PREV, halves[0], halves[1]))
    ropes = jnp.concatenate([rope, bands[BANDS][:, :ROPE]], axis=1).astype(BF)
    for k in range(NZ):
        for s in range(BANDS):
            n = s * ZBAND
            out[k, n : n + XROWS, :] = scaled[:, s * LANES : (s + 1) * LANES]
            out[k, n + XROWS : n + ZBAND, :] = bands[s].astype(BF)
        out[k, BANDS * ZBAND :, :] = ropes


def pick(first, second):
    row = lax.broadcasted_iota(jnp.int32, (PIECE, LANES), 0)
    return jnp.where(row < PREV, first.astype(F32), second.astype(F32))


def pack_kernel(ids, z_ref, out):
    bands = []
    for s in range(BANDS):
        n = s * ZBAND + XROWS
        bands.append(
            pick(z_ref[ids[4], n : n + PIECE, :], z_ref[ids[5], n : n + PIECE, :]).astype(BF)
        )
    n = BANDS * ZBAND
    last = pick(z_ref[ids[4], n : n + PIECE, :], z_ref[ids[5], n : n + PIECE, :])
    last = jnp.concatenate([last[:, ROPE:], last[:, ROPE:]], axis=1).astype(BF)
    ropes = [
        jnp.concatenate(
            [z_ref[z, n : n + XROWS, :][:, :ROPE], z_ref[z + NZ // 2, n : n + XROWS, :][:, :ROPE]],
            axis=1,
        )
        for z in range(NZ // 2)
    ]
    for k in range(NX):
        for s in range(BANDS):
            for z in range(NZ):
                first = s * XBAND + z * XROWS
                out[k, first : first + XROWS, :] = z_ref[z, s * ZBAND : s * ZBAND + XROWS, :]
            out[k, s * XBAND + SPAN : (s + 1) * XBAND, :] = bands[s]
        for z in range(NZ // 2):
            out[k, XROPE + z * XROWS : XROPE + (z + 1) * XROWS, :] = ropes[z]
        out[k, XPRE:, :] = last


def column_to_row(col):
    eye = lax.broadcasted_iota(jnp.int32, (128, 128), 0) == lax.broadcasted_iota(
        jnp.int32, (128, 128), 1
    )
    rows = [
        jnp.sum(jnp.where(eye, col[i * 128 : (i + 1) * 128, :], 0.0), axis=0, keepdims=True)
        for i in range(col.shape[0] // 128)
    ]
    return jnp.concatenate(rows, axis=0)


def row_to_column(rows):
    eye = lax.broadcasted_iota(jnp.int32, (128, 128), 0) == lax.broadcasted_iota(
        jnp.int32, (128, 128), 1
    )
    cols = [
        jnp.sum(jnp.where(eye, rows[i : i + 1, :], 0.0), axis=1, keepdims=True)
        for i in range(rows.shape[0])
    ]
    return jnp.concatenate(cols, axis=0)


def three(v):
    high = v.astype(BF).astype(F32)
    mid = (v - high).astype(BF).astype(F32)
    low = v - high - mid
    return [high, mid, low]


def attend_kernel(ids, q0, q1, q2, q3, here, there, wk, wv, out, keys, qfull, att):
    y = ids[0]
    zl = ids[6]
    c = ids[7]
    scale = 1.0 / math.sqrt(QW)
    for i, ref in enumerate((here, there)):
        for j in range(NX):
            n = (i * NX + j) * SPAN
            for s in range(BANDS):
                keys[n : n + SPAN, s * LANES : (s + 1) * LANES] = ref[
                    j, s * XBAND : s * XBAND + SPAN, :
                ]
            ropes = ref[j, XROPE:XPRE, :]
            keys[n : n + SPAN // 2, RANK:] = ropes[:, :ROPE]
            keys[n + SPAN // 2 : n + SPAN, RANK:] = ropes[:, ROPE:]
    for j in range(NX):
        n = NEW + j * PIECE
        for s in range(BANDS + 1):
            first = s * XBAND + SPAN if s < BANDS else XPRE
            mine = here[j, first : first + PIECE, :].astype(F32)
            other = there[j, first : first + PIECE, :].astype(F32)
            band = pick(
                jnp.where(ids[10] == c, mine, other), jnp.where(ids[11] == c, mine, other)
            ).astype(BF)
            if s < BANDS:
                keys[n : n + PIECE, s * LANES : (s + 1) * LANES] = band
            else:
                keys[n : n + PIECE, RANK:] = band[:, :ROPE]
    sources = (q0, q1, q2, q3)
    starts = (0, PAY, PAY, PAY)
    group = NY * TOK
    for h in range(HEADS):
        rows = jnp.concatenate(
            [q[s + h * TOK : s + (h + 1) * TOK, :] for q, s in zip(sources, starts)], axis=0
        )
        k = QROWS + h % (HEADS // 2) * TOK
        ropes = jnp.concatenate([q[s + k : s + k + TOK, :] for q, s in zip(sources, starts)], axis=0)
        ropes = ropes[:, :ROPE] if h < HEADS // 2 else ropes[:, ROPE:]
        absorbed = jnp.dot(rows, wk[h], preferred_element_type=F32).astype(BF)
        full = jnp.concatenate([absorbed, ropes], axis=1)
        qfull[h * group : (h + 1) * group, :] = full

    col = lax.broadcasted_iota(jnp.int32, (1, KEYS), 1)
    zz = lax.rem(lax.div(col, XROWS), NZ)
    xx = lax.rem(lax.div(col, XROWS * NZ), NX)
    cc = lax.div(col, XROWS * NZ * NX)
    cc = jnp.where(cc == 0, c, 1 - c)
    token = zz * (NC * TOK) + cc * TOK + xx * XROWS + lax.rem(col, XROWS) + y * (NZ * NC * TOK)
    token = jnp.where(col < NEW, token, -1)
    row = lax.rem(lax.broadcasted_iota(jnp.int32, (ROWS, 1), 0), group)
    mine = lax.rem(y + lax.div(row, TOK), NY) * (NZ * NC * TOK) + (zl * NC + c) * TOK
    visible = token <= mine + lax.rem(row, TOK)

    def score(i):
        return lax.dot_general(
            qfull[i * ROWS : (i + 1) * ROWS, :],
            keys[...],
            (((1,), (1,)), ((), ())),
            preferred_element_type=F32,
        )

    blocks = NY * QROWS // ROWS
    peaks, totals = [], []
    scores = score(0)
    for i in range(blocks):
        later = score(i + 1) if i + 1 < blocks else None
        scores = jnp.where(visible, scores, NEG)
        peak = jnp.max(scores, axis=1, keepdims=True)
        weights = jnp.exp2((scores - peak) * (scale * math.log2(math.e)))
        total = jnp.sum(weights, axis=1, keepdims=True)
        accum = jnp.dot(weights.astype(BF), keys[:, :RANK], preferred_element_type=F32)
        att[i * ROWS : (i + 1) * ROWS, :] = (accum / total).astype(BF)
        peaks.append(peak * scale)
        totals.append(total)
        scores = later
    stats = three(jnp.concatenate(peaks, axis=0)) + three(jnp.concatenate(totals, axis=0))
    for g in range(NY):
        yq = lax.rem(y + g, NY)
        parts = []
        for v in stats:
            first = [v[h * group + g * TOK : h * group + (g + 1) * TOK] for h in range(HEADS)]
            parts.append(column_to_row(jnp.concatenate(first, axis=0)))
        parts.append(jnp.zeros((STAT - 4 * len(stats), 128), F32))
        out[yq, QROWS:, :] = jnp.concatenate(parts, axis=0).astype(BF)
    for h in range(HEADS):
        mixed = jnp.dot(
            att[h * group : (h + 1) * group, :], wv[h], preferred_element_type=F32
        ).astype(BF)
        for g in range(NY):
            yq = lax.rem(y + g, NY)
            out[yq, h * TOK : (h + 1) * TOK, :] = mixed[g * TOK : (g + 1) * TOK, :]


def merge_kernel(p_ref, out, flat):
    stats = [p_ref[s, QROWS:, :].astype(F32) for s in range(NY)]
    peaks = [v[0:4] + v[4:8] + v[8:12] for v in stats]
    totals = [v[12:16] + v[16:20] + v[20:24] for v in stats]
    peak = functools.reduce(jnp.maximum, peaks)
    weights = [t * jnp.exp(p - peak) for t, p in zip(totals, peaks)]
    total = functools.reduce(jnp.add, weights)
    mixed = sum(
        p_ref[s, 0:QROWS, :].astype(F32) * row_to_column(weights[s] / total) for s in range(NY)
    )
    for h in range(HEADS):
        flat[pl.ds(h, TOK, stride=HEADS), :] = mixed[h * TOK : (h + 1) * TOK, :]
    out[...] = flat[...].reshape(TOK, HEADS, 128).astype(BF)


def on_device(
    hidden, latent_proj, norm_gain, queries, key_absorb, value_absorb, pool_blocks, hit_block
):
    y, zl, c, x = (lax.axis_index(a) for a in ("y", "zl", "c", "x"))
    owner = hit_block // POOL_HERE
    ids = jnp.concatenate(
        [
            jnp.stack([y, x]),
            owner // (NZ * NC),
            (owner // NC) % NZ,
            jnp.stack([zl, c]),
            hit_block % POOL_HERE,
            owner % NC,
        ]
    ).astype(jnp.int32)
    first = HITS * BLOCK + ((y * NZ + zl) * NC + c) * TOK
    positions = (first + jnp.arange(TOK)).astype(F32)
    half = ROPE // 2
    inverse = 10000.0 ** (-jnp.arange(half, dtype=F32) / half)
    angle = positions[:, None] * inverse[None, :]
    cosine, sine = jnp.cos(angle), jnp.sin(angle)
    cosine = jnp.concatenate([cosine, cosine], axis=1)
    sine = jnp.concatenate([-sine, sine], axis=1)

    pay = jax.ShapeDtypeStruct((PAYR, LANES), BF)
    own_q, own_p, p1, p2, p3 = pl.pallas_call(
        prepare_kernel,
        out_shape=[
            jax.ShapeDtypeStruct((PAYR - PAY, LANES), BF),
            jax.ShapeDtypeStruct((PAY, LANES), BF),
            pay,
            pay,
            pay,
        ],
        in_specs=[SMEM] + [VMEM] * 3 + [pl.BlockSpec(memory_space=pltpu.HBM)],
        out_specs=[VMEM] * 5,
        scratch_shapes=[
            pltpu.VMEM((QROWS, 128), F32),
            pltpu.VMEM((QROWS, 128), F32),
            pltpu.VMEM((HITS, WIDTH, BLOCK), BF),
            pltpu.VMEM((HITS * BLOCK, WIDTH), F32),
            pltpu.SemaphoreType.DMA((HITS,)),
        ],
        compiler_params=params(),
        name="prepare",
    )(hit_block, queries, cosine, sine, jnp.swapaxes(pool_blocks, 1, 2))
    received = [
        lax.ppermute(p, "y", [(i, (i - k) % NY) for i in range(NY)])
        for k, p in zip((1, 2, 3), (p1, p2, p3))
    ]

    hidden, own_p = lax.optimization_barrier((hidden, own_p))
    partial = pl.pallas_call(
        project_kernel,
        out_shape=jax.ShapeDtypeStruct((NX, RAWR, LANES), F32),
        in_specs=[VMEM] * 2,
        out_specs=VMEM,
        compiler_params=params(),
        name="project",
    )(hidden, latent_proj.T)
    mine = jnp.sum(lax.all_to_all(partial, "x", 0, 0), axis=0)
    other = lax.ppermute(mine, "zh", [(0, 1), (1, 0)])
    head = pl.BlockSpec((PAY, LANES), lambda i: (0, 0))

    def whole(shape):
        return pl.BlockSpec(shape, lambda i: (0,) * len(shape))

    packed = pl.pallas_call(
        norm_kernel,
        grid=(1,),
        out_shape=jax.ShapeDtypeStruct((NZ, ZROWS, LANES), BF),
        in_specs=[
            SMEM,
            whole((RAWR, LANES)),
            whole((RAWR, LANES)),
            whole((1, RANK)),
            whole((TOK, ROPE)),
            whole((TOK, ROPE)),
            head,
            head,
            head,
            head,
        ],
        out_specs=whole((NZ, ZROWS, LANES)),
        compiler_params=params(),
        name="norm",
    )(ids, mine, other, norm_gain[None, :], cosine, sine, own_p, *received)
    along_z = lax.all_to_all(packed, "zl", 0, 0)
    packed = pl.pallas_call(
        pack_kernel,
        out_shape=jax.ShapeDtypeStruct((NX, CHUNK, LANES), BF),
        in_specs=[SMEM, VMEM],
        out_specs=VMEM,
        compiler_params=params(),
        name="pack",
    )(ids, along_z)
    along_x = lax.all_to_all(packed, "x", 0, 0)
    from_core = lax.ppermute(along_x, "c", [(0, 1), (1, 0)])
    out = pl.pallas_call(
        attend_kernel,
        out_shape=jax.ShapeDtypeStruct((NY, OUTR, 128), BF),
        in_specs=[SMEM] + [VMEM] * 8,
        out_specs=VMEM,
        scratch_shapes=[
            pltpu.VMEM((KEYS, WIDTH), BF),
            pltpu.VMEM((NY * QROWS, WIDTH), BF),
            pltpu.VMEM((NY * QROWS, RANK), BF),
        ],
        compiler_params=params(48),
        name="attend",
    )(ids, own_q, *received, along_x, from_core, key_absorb, value_absorb)
    back = lax.all_to_all(out, "y", 0, 0)
    return pl.pallas_call(
        merge_kernel,
        out_shape=jax.ShapeDtypeStruct((TOK, HEADS, 128), BF),
        in_specs=[VMEM],
        out_specs=VMEM,
        scratch_shapes=[pltpu.VMEM((QROWS, 128), F32)],
        compiler_params=params(),
        name="merge",
    )(back)


def solution(mesh):
    fine = Mesh(mesh.devices.reshape(NY, NZ, NC, NH, NX), CTX + HEAD)
    placed = (
        P(CTX, HEAD),
        P(HEAD, None),
        P(),
        P(CTX, HEAD, None),
        P(HEAD, None, None),
        P(HEAD, None, None),
        P(CTX, None, None),
        P(),
    )
    return jax.shard_map(
        on_device, mesh=fine, in_specs=placed, out_specs=P(CTX, HEAD, None), check_vma=False
    )
```

```python
import functools
import math

import jax
import jax.numpy as jnp
from jax import lax
from jax.experimental import pallas as pl
from jax.experimental.pallas import tpu as pltpu
from jax.sharding import Mesh, PartitionSpec as P

EPS = 1e-06
NEG = -1e30
BF = jnp.bfloat16
F32 = jnp.float32

NY, NZ, NC, NH, NX = 4, 8, 2, 2, 4
CTX = ("y", "zl", "c")
HEAD = ("zh", "x")

TOK = 64
RANK = 512
WIDTH = 576
NOPE = 128
ROPE = 64
QW = 192
HEADS = 8
BLOCK = 128
POOL_HERE = 4
HITS = 2
XROWS = TOK // NX
PREV = 8
PIECE = HITS * PREV
QROWS = TOK * HEADS
LANES = 128
ATT_MIB = 28
PROJ_MIB = 62
BANDS = RANK // LANES
PAY = (BANDS + 1) * PIECE
PAYQ = PAY + QROWS
PAYR = PAYQ + QROWS // 2
RAWR = BANDS * XROWS + XROWS // 2
ZBAND = XROWS + PIECE
ZROWS = BANDS * ZBAND + 16
SPAN = NZ * XROWS
XBAND = SPAN + PIECE
XROPE = BANDS * XBAND
XPRE = XROPE + SPAN // 2
CHUNK = XPRE + PIECE
NEW = NC * NX * NZ * XROWS
PRE = NX * PIECE
KEYS = NEW + PRE
STAT = 32
OUTR = QROWS + STAT
ROWS = 512

VMEM = pl.BlockSpec(memory_space=pltpu.VMEM)
SMEM = pl.BlockSpec(memory_space=pltpu.SMEM)


def params(mib=32):
    return pltpu.CompilerParams(vmem_limit_bytes=mib * 2**20)


def swap_halves(v):
    half = v.shape[-1] // 2
    return jnp.concatenate([v[:, half:], v[:, :half]], axis=1)


def prepare_kernel(hit, q_ref, cos_ref, sin_ref, pool_ref, out, qn, qr, found, pre, sem):
    x = lax.axis_index("x")
    copies = [
        pltpu.make_async_copy(pool_ref.at[lax.rem(hit[b], POOL_HERE)], found.at[b], sem.at[b])
        for b in range(HITS)
    ]
    for copy in copies:
        copy.start()
    flat = q_ref[...].astype(F32).reshape(QROWS, QW)
    qn[...] = flat[:, :NOPE]
    qr[:, :ROPE] = flat[:, NOPE:]
    cosine = cos_ref[...]
    sine = sin_ref[...]
    ropes = []
    for h in range(HEADS):
        rope = qr[pl.ds(h, TOK, stride=HEADS), :][:, :ROPE]
        ropes.append(rope * cosine + swap_halves(rope) * sine)
        rows = qn[pl.ds(h, TOK, stride=HEADS), :].astype(BF)
        for g in range(NY):
            out[g, PAY + h * TOK : PAY + (h + 1) * TOK, :] = rows
    for h in range(HEADS // 2):
        rows = jnp.concatenate([ropes[h], ropes[h + HEADS // 2]], axis=1).astype(BF)
        for g in range(NY):
            out[g, PAYQ + h * TOK : PAYQ + (h + 1) * TOK, :] = rows
    for b in range(HITS):
        copies[b].wait()
        pre[b * BLOCK : (b + 1) * BLOCK, :] = found[b].astype(F32).T
    quarter = BLOCK // NX
    blocks = [
        pre[pl.ds(pl.multiple_of(b * BLOCK + x * quarter, quarter), quarter), :]
        for b in range(HITS)
    ]
    for g in range(NY):
        piece = jnp.concatenate([v[g * PREV : (g + 1) * PREV] for v in blocks], axis=0)
        piece = jnp.concatenate([piece, piece[:, RANK:]], axis=1).astype(BF)
        for s in range(BANDS + 1):
            out[g, s * PIECE : (s + 1) * PIECE, :] = piece[:, s * LANES : (s + 1) * LANES]


def project_kernel(hidden, proj, out):
    partial = lax.dot_general(
        hidden[...], proj[...], (((1,), (1,)), ((), ())), preferred_element_type=F32
    )
    for k in range(NX):
        rows = partial[k * XROWS : (k + 1) * XROWS]
        for s in range(BANDS):
            out[k, s * XROWS : (s + 1) * XROWS, :] = rows[:, s * LANES : (s + 1) * LANES]
        rope = rows[:, RANK:]
        half = XROWS // 2
        out[k, BANDS * XROWS :, :] = jnp.concatenate([rope[:half], rope[half:]], axis=1)


def norm_kernel(ids, s_ref, r_ref, gain_ref, cos_ref, sin_ref, p_ref, out):
    x = ids[1]
    raw = s_ref[...] + r_ref[...]
    latent = jnp.concatenate([raw[s * XROWS : (s + 1) * XROWS] for s in range(BANDS)], axis=1)
    rope = raw[BANDS * XROWS :]
    rope = jnp.concatenate([rope[:, :ROPE], rope[:, ROPE:]], axis=0)
    mean = jnp.mean(latent * latent, axis=1, keepdims=True)
    scaled = (latent * lax.rsqrt(mean + EPS) * gain_ref[...]).astype(BF)
    start = pl.multiple_of(x * XROWS, XROWS)
    cosine = cos_ref[pl.ds(start, XROWS), :]
    sine = sin_ref[pl.ds(start, XROWS), :]
    rope = rope * cosine + swap_halves(rope) * sine
    row = lax.broadcasted_iota(jnp.int32, (PIECE, LANES), 0)
    bands = []
    for s in range(BANDS + 1):
        first = p_ref[ids[2], s * PIECE : (s + 1) * PIECE, :].astype(F32)
        second = p_ref[ids[3], s * PIECE : (s + 1) * PIECE, :].astype(F32)
        bands.append(jnp.where(row < PREV, first, second))
    ropes = jnp.concatenate([rope, bands[BANDS][:, :ROPE]], axis=1).astype(BF)
    for k in range(NZ):
        for s in range(BANDS):
            n = s * ZBAND
            out[k, n : n + XROWS, :] = scaled[:, s * LANES : (s + 1) * LANES]
            out[k, n + XROWS : n + ZBAND, :] = bands[s].astype(BF)
        out[k, BANDS * ZBAND :, :] = ropes


def pick(first, second):
    row = lax.broadcasted_iota(jnp.int32, (PIECE, LANES), 0)
    return jnp.where(row < PREV, first.astype(F32), second.astype(F32))


def pack_kernel(ids, z_ref, out):
    bands = []
    for s in range(BANDS):
        n = s * ZBAND + XROWS
        bands.append(
            pick(z_ref[ids[4], n : n + PIECE, :], z_ref[ids[5], n : n + PIECE, :]).astype(BF)
        )
    n = BANDS * ZBAND
    last = pick(z_ref[ids[4], n : n + PIECE, :], z_ref[ids[5], n : n + PIECE, :])
    last = jnp.concatenate([last[:, ROPE:], last[:, ROPE:]], axis=1).astype(BF)
    ropes = [
        jnp.concatenate(
            [z_ref[z, n : n + XROWS, :][:, :ROPE], z_ref[z + NZ // 2, n : n + XROWS, :][:, :ROPE]],
            axis=1,
        )
        for z in range(NZ // 2)
    ]
    for k in range(NX):
        for s in range(BANDS):
            for z in range(NZ):
                first = s * XBAND + z * XROWS
                out[k, first : first + XROWS, :] = z_ref[z, s * ZBAND : s * ZBAND + XROWS, :]
            out[k, s * XBAND + SPAN : (s + 1) * XBAND, :] = bands[s]
        for z in range(NZ // 2):
            out[k, XROPE + z * XROWS : XROPE + (z + 1) * XROWS, :] = ropes[z]
        out[k, XPRE:, :] = last


def column_to_row(col):
    eye = lax.broadcasted_iota(jnp.int32, (128, 128), 0) == lax.broadcasted_iota(
        jnp.int32, (128, 128), 1
    )
    rows = [
        jnp.sum(jnp.where(eye, col[i * 128 : (i + 1) * 128, :], 0.0), axis=0, keepdims=True)
        for i in range(col.shape[0] // 128)
    ]
    return jnp.concatenate(rows, axis=0)


def row_to_column(rows):
    eye = lax.broadcasted_iota(jnp.int32, (128, 128), 0) == lax.broadcasted_iota(
        jnp.int32, (128, 128), 1
    )
    cols = [
        jnp.sum(jnp.where(eye, rows[i : i + 1, :], 0.0), axis=1, keepdims=True)
        for i in range(rows.shape[0])
    ]
    return jnp.concatenate(cols, axis=0)


def three(v):
    high = v.astype(BF).astype(F32)
    mid = (v - high).astype(BF).astype(F32)
    low = v - high - mid
    return [high, mid, low]


def absorb_kernel(q_ref, wk, qfull):
    group = NY * TOK
    for h in range(HEADS):
        k = PAY + h * TOK
        rows = jnp.concatenate([q_ref[g, k : k + TOK, :] for g in range(NY)], axis=0)
        k = PAYQ + h % (HEADS // 2) * TOK
        ropes = jnp.concatenate([q_ref[g, k : k + TOK, :] for g in range(NY)], axis=0)
        ropes = ropes[:, :ROPE] if h < HEADS // 2 else ropes[:, ROPE:]
        absorbed = jnp.dot(rows, wk[h], preferred_element_type=F32).astype(BF)
        full = jnp.concatenate([absorbed, ropes], axis=1)
        qfull[h * group : (h + 1) * group, :] = full


def attend_kernel(ids, qfull, here, there, wv, out, keys, att):
    y = ids[0]
    zl = ids[6]
    c = ids[7]
    scale = 1.0 / math.sqrt(QW)
    for i, ref in enumerate((here, there)):
        for j in range(NX):
            n = (i * NX + j) * SPAN
            for s in range(BANDS):
                keys[n : n + SPAN, s * LANES : (s + 1) * LANES] = ref[
                    j, s * XBAND : s * XBAND + SPAN, :
                ]
            ropes = ref[j, XROPE:XPRE, :]
            keys[n : n + SPAN // 2, RANK:] = ropes[:, :ROPE]
            keys[n + SPAN // 2 : n + SPAN, RANK:] = ropes[:, ROPE:]
    for j in range(NX):
        n = NEW + j * PIECE
        for s in range(BANDS + 1):
            first = s * XBAND + SPAN if s < BANDS else XPRE
            mine = here[j, first : first + PIECE, :].astype(F32)
            other = there[j, first : first + PIECE, :].astype(F32)
            band = pick(
                jnp.where(ids[10] == c, mine, other), jnp.where(ids[11] == c, mine, other)
            ).astype(BF)
            if s < BANDS:
                keys[n : n + PIECE, s * LANES : (s + 1) * LANES] = band
            else:
                keys[n : n + PIECE, RANK:] = band[:, :ROPE]
    group = NY * TOK
    col = lax.broadcasted_iota(jnp.int32, (1, KEYS), 1)
    zz = lax.rem(lax.div(col, XROWS), NZ)
    xx = lax.rem(lax.div(col, XROWS * NZ), NX)
    cc = lax.div(col, XROWS * NZ * NX)
    cc = jnp.where(cc == 0, c, 1 - c)
    token = zz * (NC * TOK) + cc * TOK + xx * XROWS + lax.rem(col, XROWS) + y * (NZ * NC * TOK)
    token = jnp.where(col < NEW, token, -1)
    row = lax.rem(lax.broadcasted_iota(jnp.int32, (ROWS, 1), 0), group)
    mine = lax.div(row, TOK) * (NZ * NC * TOK) + (zl * NC + c) * TOK
    visible = token <= mine + lax.rem(row, TOK)

    def score(i):
        return lax.dot_general(
            qfull[i * ROWS : (i + 1) * ROWS, :],
            keys[...],
            (((1,), (1,)), ((), ())),
            preferred_element_type=F32,
        )

    blocks = NY * QROWS // ROWS
    peaks, totals = [], []
    scores = score(0)
    for i in range(blocks):
        later = score(i + 1) if i + 1 < blocks else None
        scores = jnp.where(visible, scores, NEG)
        peak = jnp.max(scores, axis=1, keepdims=True)
        weights = jnp.exp2((scores - peak) * (scale * math.log2(math.e)))
        total = jnp.sum(weights, axis=1, keepdims=True)
        accum = jnp.dot(weights.astype(BF), keys[:, :RANK], preferred_element_type=F32)
        att[i * ROWS : (i + 1) * ROWS, :] = (accum / total).astype(BF)
        peaks.append(peak * scale)
        totals.append(total)
        scores = later
    stats = three(jnp.concatenate(peaks, axis=0)) + three(jnp.concatenate(totals, axis=0))
    for g in range(NY):
        parts = []
        for v in stats:
            first = [v[h * group + g * TOK : h * group + (g + 1) * TOK] for h in range(HEADS)]
            parts.append(column_to_row(jnp.concatenate(first, axis=0)))
        parts.append(jnp.zeros((STAT - 4 * len(stats), 128), F32))
        out[g, QROWS:, :] = jnp.concatenate(parts, axis=0).astype(BF)
    for h in range(HEADS):
        mixed = jnp.dot(
            att[h * group : (h + 1) * group, :], wv[h], preferred_element_type=F32
        ).astype(BF)
        for g in range(NY):
            out[g, h * TOK : (h + 1) * TOK, :] = mixed[g * TOK : (g + 1) * TOK, :]


def merge_kernel(p_ref, out, flat):
    stats = [p_ref[s, QROWS:, :].astype(F32) for s in range(NY)]
    peaks = [v[0:4] + v[4:8] + v[8:12] for v in stats]
    totals = [v[12:16] + v[16:20] + v[20:24] for v in stats]
    peak = functools.reduce(jnp.maximum, peaks)
    weights = [t * jnp.exp(p - peak) for t, p in zip(totals, peaks)]
    total = functools.reduce(jnp.add, weights)
    mixed = sum(
        p_ref[s, 0:QROWS, :].astype(F32) * row_to_column(weights[s] / total) for s in range(NY)
    )
    for h in range(HEADS):
        flat[pl.ds(h, TOK, stride=HEADS), :] = mixed[h * TOK : (h + 1) * TOK, :]
    out[...] = flat[...].reshape(TOK, HEADS, 128).astype(BF)


def on_device(
    hidden, latent_proj, norm_gain, queries, key_absorb, value_absorb, pool_blocks, hit_block
):
    y, zl, c, x = (lax.axis_index(a) for a in ("y", "zl", "c", "x"))
    owner = hit_block // POOL_HERE
    ids = jnp.concatenate(
        [
            jnp.stack([y, x]),
            owner // (NZ * NC),
            (owner // NC) % NZ,
            jnp.stack([zl, c]),
            hit_block % POOL_HERE,
            owner % NC,
        ]
    ).astype(jnp.int32)
    first = HITS * BLOCK + ((y * NZ + zl) * NC + c) * TOK
    positions = (first + jnp.arange(TOK)).astype(F32)
    half = ROPE // 2
    inverse = 10000.0 ** (-jnp.arange(half, dtype=F32) / half)
    angle = positions[:, None] * inverse[None, :]
    cosine, sine = jnp.cos(angle), jnp.sin(angle)
    cosine = jnp.concatenate([cosine, cosine], axis=1)
    sine = jnp.concatenate([-sine, sine], axis=1)

    sent = pl.pallas_call(
        prepare_kernel,
        out_shape=jax.ShapeDtypeStruct((NY, PAYR, LANES), BF),
        in_specs=[SMEM] + [VMEM] * 3 + [pl.BlockSpec(memory_space=pltpu.HBM)],
        out_specs=VMEM,
        scratch_shapes=[
            pltpu.VMEM((QROWS, 128), F32),
            pltpu.VMEM((QROWS, 128), F32),
            pltpu.VMEM((HITS, WIDTH, BLOCK), BF),
            pltpu.VMEM((HITS * BLOCK, WIDTH), F32),
            pltpu.SemaphoreType.DMA((HITS,)),
        ],
        compiler_params=params(),
        name="prepare",
    )(hit_block, queries, cosine, sine, jnp.swapaxes(pool_blocks, 1, 2))
    received = lax.all_to_all(sent, "y", 0, 0)

    partial = pl.pallas_call(
        project_kernel,
        out_shape=jax.ShapeDtypeStruct((NX, RAWR, LANES), F32),
        in_specs=[VMEM] * 2,
        out_specs=VMEM,
        compiler_params=params(PROJ_MIB),
        name="project",
    )(hidden, latent_proj.T)
    mine = jnp.sum(lax.all_to_all(partial, "x", 0, 0), axis=0)
    other = lax.ppermute(mine, "zh", [(0, 1), (1, 0)])
    def whole(shape):
        return pl.BlockSpec(shape, lambda i: (0,) * len(shape))

    packed = pl.pallas_call(
        norm_kernel,
        grid=(1,),
        out_shape=jax.ShapeDtypeStruct((NZ, ZROWS, LANES), BF),
        in_specs=[
            SMEM,
            whole((RAWR, LANES)),
            whole((RAWR, LANES)),
            whole((1, RANK)),
            whole((TOK, ROPE)),
            whole((TOK, ROPE)),
            whole((NY, PAY, LANES)),
        ],
        out_specs=whole((NZ, ZROWS, LANES)),
        compiler_params=params(),
        name="norm",
    )(ids, mine, other, norm_gain[None, :], cosine, sine, received)
    along_z = lax.all_to_all(packed, "zl", 0, 0)
    packed = pl.pallas_call(
        pack_kernel,
        out_shape=jax.ShapeDtypeStruct((NX, CHUNK, LANES), BF),
        in_specs=[SMEM, VMEM],
        out_specs=VMEM,
        compiler_params=params(),
        name="pack",
    )(ids, along_z)
    along_x = lax.all_to_all(packed, "x", 0, 0)
    from_core = lax.ppermute(along_x, "c", [(0, 1), (1, 0)])
    qfull = pl.pallas_call(
        absorb_kernel,
        out_shape=jax.ShapeDtypeStruct((NY * QROWS, WIDTH), BF),
        in_specs=[VMEM] * 2,
        out_specs=VMEM,
        compiler_params=params(16),
        name="absorb",
    )(received, key_absorb)
    out = pl.pallas_call(
        attend_kernel,
        out_shape=jax.ShapeDtypeStruct((NY, OUTR, 128), BF),
        in_specs=[SMEM] + [VMEM] * 4,
        out_specs=VMEM,
        scratch_shapes=[
            pltpu.VMEM((KEYS, WIDTH), BF),
            pltpu.VMEM((NY * QROWS, RANK), BF),
        ],
        compiler_params=params(ATT_MIB),
        name="attend",
    )(ids, qfull, along_x, from_core, value_absorb)
    back = lax.all_to_all(out, "y", 0, 0)
    return pl.pallas_call(
        merge_kernel,
        out_shape=jax.ShapeDtypeStruct((TOK, HEADS, 128), BF),
        in_specs=[VMEM],
        out_specs=VMEM,
        scratch_shapes=[pltpu.VMEM((QROWS, 128), F32)],
        compiler_params=params(),
        name="merge",
    )(back)


def solution(mesh):
    fine = Mesh(mesh.devices.reshape(NY, NZ, NC, NH, NX), CTX + HEAD)
    placed = (
        P(CTX, HEAD),
        P(HEAD, None),
        P(),
        P(CTX, HEAD, None),
        P(HEAD, None, None),
        P(HEAD, None, None),
        P(CTX, None, None),
        P(),
    )
    return jax.shard_map(
        on_device, mesh=fine, in_specs=placed, out_specs=P(CTX, HEAD, None), check_vma=False
    )
```

```python
import functools
import math

import jax
import jax.numpy as jnp
from jax import lax
from jax.experimental import pallas as pl
from jax.experimental.pallas import tpu as pltpu
from jax.sharding import Mesh, PartitionSpec as P

EPS = 1e-06
NEG = -1e30
BF = jnp.bfloat16
F32 = jnp.float32

NY, NZ, NC, NH, NX = 4, 8, 2, 2, 4
NR = NZ // 2
CTX = ("y", "zq", "zr", "c")
HEAD = ("zh", "x")

TOK = 64
RANK = 512
WIDTH = 576
NOPE = 128
ROPE = 64
QW = 192
HEADS = 8
BLOCK = 128
POOL_HERE = 4
HITS = 2
XROWS = TOK // NX
PREV = 8
PIECE = HITS * PREV
QROWS = TOK * HEADS
LANES = 128
ATT_MIB = 28
PROJ_MIB = 62
BANDS = RANK // LANES
PAY = (BANDS + 1) * PIECE
PAYQ = PAY + QROWS
PAYR = PAYQ + QROWS // 2
RAWR = BANDS * XROWS + XROWS // 2
ZBAND = XROWS + PIECE
ZROWS = BANDS * ZBAND + 16
HALF = NR * XROWS
HBAND = HALF + PIECE
HROPE = BANDS * HBAND
HPRE = HROPE + HALF // 2
HROWS = HPRE + PIECE
SPAN = NZ * XROWS
XBAND = SPAN + PIECE
XROPE = BANDS * XBAND
XPRE = XROPE + SPAN // 2
CHUNK = XPRE + PIECE
NEW = NC * NX * NZ * XROWS
PRE = NX * PIECE
KEYS = NEW + PRE
STAT = 32
OUTR = QROWS + STAT
ROWS = 512

VMEM = pl.BlockSpec(memory_space=pltpu.VMEM)
SMEM = pl.BlockSpec(memory_space=pltpu.SMEM)


def params(mib=32):
    return pltpu.CompilerParams(vmem_limit_bytes=mib * 2**20)


def swap_halves(v):
    half = v.shape[-1] // 2
    return jnp.concatenate([v[:, half:], v[:, :half]], axis=1)


def prepare_kernel(hit, q_ref, cos_ref, sin_ref, pool_ref, out, qn, qr, found, pre, sem):
    x = lax.axis_index("x")
    copies = [
        pltpu.make_async_copy(pool_ref.at[lax.rem(hit[b], POOL_HERE)], found.at[b], sem.at[b])
        for b in range(HITS)
    ]
    for copy in copies:
        copy.start()
    flat = q_ref[...].astype(F32).reshape(QROWS, QW)
    qn[...] = flat[:, :NOPE]
    qr[:, :ROPE] = flat[:, NOPE:]
    cosine = cos_ref[...]
    sine = sin_ref[...]
    ropes = []
    for h in range(HEADS):
        rope = qr[pl.ds(h, TOK, stride=HEADS), :][:, :ROPE]
        ropes.append(rope * cosine + swap_halves(rope) * sine)
        rows = qn[pl.ds(h, TOK, stride=HEADS), :].astype(BF)
        for g in range(NY):
            out[g, PAY + h * TOK : PAY + (h + 1) * TOK, :] = rows
    for h in range(HEADS // 2):
        rows = jnp.concatenate([ropes[h], ropes[h + HEADS // 2]], axis=1).astype(BF)
        for g in range(NY):
            out[g, PAYQ + h * TOK : PAYQ + (h + 1) * TOK, :] = rows
    for b in range(HITS):
        copies[b].wait()
        pre[b * BLOCK : (b + 1) * BLOCK, :] = found[b].astype(F32).T
    quarter = BLOCK // NX
    blocks = [
        pre[pl.ds(pl.multiple_of(b * BLOCK + x * quarter, quarter), quarter), :]
        for b in range(HITS)
    ]
    for g in range(NY):
        piece = jnp.concatenate([v[g * PREV : (g + 1) * PREV] for v in blocks], axis=0)
        piece = jnp.concatenate([piece, piece[:, RANK:]], axis=1).astype(BF)
        for s in range(BANDS + 1):
            out[g, s * PIECE : (s + 1) * PIECE, :] = piece[:, s * LANES : (s + 1) * LANES]


def project_kernel(hidden, proj, out):
    partial = lax.dot_general(
        hidden[...], proj[...], (((1,), (1,)), ((), ())), preferred_element_type=F32
    )
    for k in range(NX):
        rows = partial[k * XROWS : (k + 1) * XROWS]
        for s in range(BANDS):
            out[k, s * XROWS : (s + 1) * XROWS, :] = rows[:, s * LANES : (s + 1) * LANES]
        rope = rows[:, RANK:]
        half = XROWS // 2
        out[k, BANDS * XROWS :, :] = jnp.concatenate([rope[:half], rope[half:]], axis=1)


def norm_kernel(ids, s_ref, r_ref, gain_ref, cos_ref, sin_ref, p_ref, out):
    x = ids[1]
    raw = s_ref[...] + r_ref[...]
    latent = jnp.concatenate([raw[s * XROWS : (s + 1) * XROWS] for s in range(BANDS)], axis=1)
    rope = raw[BANDS * XROWS :]
    rope = jnp.concatenate([rope[:, :ROPE], rope[:, ROPE:]], axis=0)
    mean = jnp.mean(latent * latent, axis=1, keepdims=True)
    scaled = (latent * lax.rsqrt(mean + EPS) * gain_ref[...]).astype(BF)
    start = pl.multiple_of(x * XROWS, XROWS)
    cosine = cos_ref[pl.ds(start, XROWS), :]
    sine = sin_ref[pl.ds(start, XROWS), :]
    rope = rope * cosine + swap_halves(rope) * sine
    row = lax.broadcasted_iota(jnp.int32, (PIECE, LANES), 0)
    bands = []
    for s in range(BANDS + 1):
        first = p_ref[ids[2], s * PIECE : (s + 1) * PIECE, :].astype(F32)
        second = p_ref[ids[3], s * PIECE : (s + 1) * PIECE, :].astype(F32)
        bands.append(jnp.where(row < PREV, first, second))
    ropes = jnp.concatenate([rope, bands[BANDS][:, :ROPE]], axis=1).astype(BF)
    for k in range(NR):
        for s in range(BANDS):
            n = s * ZBAND
            out[k, n : n + XROWS, :] = scaled[:, s * LANES : (s + 1) * LANES]
            out[k, n + XROWS : n + ZBAND, :] = bands[s].astype(BF)
        out[k, BANDS * ZBAND :, :] = ropes


def pick(first, second):
    row = lax.broadcasted_iota(jnp.int32, (PIECE, LANES), 0)
    return jnp.where(row < PREV, first.astype(F32), second.astype(F32))


def half_kernel(ids, z_ref, out):
    first, second = lax.rem(ids[4], NR), lax.rem(ids[5], NR)
    n = BANDS * ZBAND
    for s in range(BANDS):
        for k in range(NR):
            m = s * HBAND + k * XROWS
            out[m : m + XROWS, :] = z_ref[k, s * ZBAND : s * ZBAND + XROWS, :]
        m = s * ZBAND + XROWS
        band = pick(z_ref[first, m : m + PIECE, :], z_ref[second, m : m + PIECE, :])
        out[s * HBAND + HALF : (s + 1) * HBAND, :] = band.astype(BF)
    for k in range(NR // 2):
        m = HROPE + k * XROWS
        out[m : m + XROWS, :] = jnp.concatenate(
            [z_ref[i, n : n + XROWS, :][:, :ROPE] for i in (k, k + NR // 2)], axis=1
        )
    band = pick(z_ref[first, n : n + PIECE, :], z_ref[second, n : n + PIECE, :])
    out[HPRE:, :] = jnp.concatenate([band[:, ROPE:], band[:, ROPE:]], axis=1).astype(BF)


def pack_kernel(ids, own, other, out):
    quad = lax.div(ids[6], NR)
    mine = [lax.div(ids[4 + b], NR) == quad for b in range(HITS)]

    def piece(m):
        a = own[m : m + PIECE, :].astype(F32)
        b = other[m : m + PIECE, :].astype(F32)
        return pick(*[jnp.where(here, a, b) for here in mine]).astype(BF)

    bands = [piece(s * HBAND + HALF) for s in range(BANDS)]
    last = piece(HPRE)
    for k in range(NX):
        for i, ref in enumerate((own, other)):
            for s in range(BANDS):
                n = s * XBAND + i * HALF
                out[k, n : n + HALF, :] = ref[s * HBAND : s * HBAND + HALF, :]
            n = XROPE + i * (HALF // 2)
            out[k, n : n + HALF // 2, :] = ref[HROPE:HPRE, :]
        for s in range(BANDS):
            out[k, s * XBAND + SPAN : (s + 1) * XBAND, :] = bands[s]
        out[k, XPRE:, :] = last


def column_to_row(col):
    eye = lax.broadcasted_iota(jnp.int32, (128, 128), 0) == lax.broadcasted_iota(
        jnp.int32, (128, 128), 1
    )
    rows = [
        jnp.sum(jnp.where(eye, col[i * 128 : (i + 1) * 128, :], 0.0), axis=0, keepdims=True)
        for i in range(col.shape[0] // 128)
    ]
    return jnp.concatenate(rows, axis=0)


def row_to_column(rows):
    eye = lax.broadcasted_iota(jnp.int32, (128, 128), 0) == lax.broadcasted_iota(
        jnp.int32, (128, 128), 1
    )
    cols = [
        jnp.sum(jnp.where(eye, rows[i : i + 1, :], 0.0), axis=1, keepdims=True)
        for i in range(rows.shape[0])
    ]
    return jnp.concatenate(cols, axis=0)


def three(v):
    high = v.astype(BF).astype(F32)
    mid = (v - high).astype(BF).astype(F32)
    low = v - high - mid
    return [high, mid, low]


def absorb_kernel(q_ref, wk, qfull):
    group = NY * TOK
    for h in range(HEADS):
        k = PAY + h * TOK
        rows = jnp.concatenate([q_ref[g, k : k + TOK, :] for g in range(NY)], axis=0)
        k = PAYQ + h % (HEADS // 2) * TOK
        ropes = jnp.concatenate([q_ref[g, k : k + TOK, :] for g in range(NY)], axis=0)
        ropes = ropes[:, :ROPE] if h < HEADS // 2 else ropes[:, ROPE:]
        absorbed = jnp.dot(rows, wk[h], preferred_element_type=F32).astype(BF)
        full = jnp.concatenate([absorbed, ropes], axis=1)
        qfull[h * group : (h + 1) * group, :] = full


def attend_kernel(ids, qfull, here, there, wv, out, keys, att):
    y = ids[0]
    zl = ids[6]
    c = ids[7]
    scale = 1.0 / math.sqrt(QW)
    for i, ref in enumerate((here, there)):
        for j in range(NX):
            n = (i * NX + j) * SPAN
            for s in range(BANDS):
                keys[n : n + SPAN, s * LANES : (s + 1) * LANES] = ref[
                    j, s * XBAND : s * XBAND + SPAN, :
                ]
            ropes = ref[j, XROPE:XPRE, :]
            for k in range(4):
                m = k // 2 * (HALF // 2)
                part = ropes[m : m + HALF // 2]
                part = part[:, :ROPE] if k % 2 == 0 else part[:, ROPE:]
                keys[n + k * (HALF // 2) : n + (k + 1) * (HALF // 2), RANK:] = part
    for j in range(NX):
        n = NEW + j * PIECE
        for s in range(BANDS + 1):
            first = s * XBAND + SPAN if s < BANDS else XPRE
            mine = here[j, first : first + PIECE, :].astype(F32)
            other = there[j, first : first + PIECE, :].astype(F32)
            band = pick(
                jnp.where(ids[10] == c, mine, other), jnp.where(ids[11] == c, mine, other)
            ).astype(BF)
            if s < BANDS:
                keys[n : n + PIECE, s * LANES : (s + 1) * LANES] = band
            else:
                keys[n : n + PIECE, RANK:] = band[:, :ROPE]
    group = NY * TOK
    col = lax.broadcasted_iota(jnp.int32, (1, KEYS), 1)
    slot = lax.rem(lax.div(col, XROWS), NZ)
    quad = lax.div(zl, NR)
    zz = jnp.where(slot < NR, quad, 1 - quad) * NR + lax.rem(slot, NR)
    xx = lax.rem(lax.div(col, XROWS * NZ), NX)
    cc = lax.div(col, XROWS * NZ * NX)
    cc = jnp.where(cc == 0, c, 1 - c)
    token = zz * (NC * TOK) + cc * TOK + xx * XROWS + lax.rem(col, XROWS) + y * (NZ * NC * TOK)
    token = jnp.where(col < NEW, token, -1)
    row = lax.rem(lax.broadcasted_iota(jnp.int32, (ROWS, 1), 0), group)
    mine = lax.div(row, TOK) * (NZ * NC * TOK) + (zl * NC + c) * TOK
    visible = token <= mine + lax.rem(row, TOK)

    def score(i):
        return lax.dot_general(
            qfull[i * ROWS : (i + 1) * ROWS, :],
            keys[...],
            (((1,), (1,)), ((), ())),
            preferred_element_type=F32,
        )

    blocks = NY * QROWS // ROWS
    peaks, totals = [], []
    scores = score(0)
    for i in range(blocks):
        later = score(i + 1) if i + 1 < blocks else None
        scores = jnp.where(visible, scores, NEG)
        peak = jnp.max(scores, axis=1, keepdims=True)
        weights = jnp.exp2((scores - peak) * (scale * math.log2(math.e)))
        total = jnp.sum(weights, axis=1, keepdims=True)
        accum = jnp.dot(weights.astype(BF), keys[:, :RANK], preferred_element_type=F32)
        att[i * ROWS : (i + 1) * ROWS, :] = (accum / total).astype(BF)
        peaks.append(peak * scale)
        totals.append(total)
        scores = later
    stats = three(jnp.concatenate(peaks, axis=0)) + three(jnp.concatenate(totals, axis=0))
    for g in range(NY):
        parts = []
        for v in stats:
            first = [v[h * group + g * TOK : h * group + (g + 1) * TOK] for h in range(HEADS)]
            parts.append(column_to_row(jnp.concatenate(first, axis=0)))
        parts.append(jnp.zeros((STAT - 4 * len(stats), 128), F32))
        out[g, QROWS:, :] = jnp.concatenate(parts, axis=0).astype(BF)
    for h in range(HEADS):
        mixed = jnp.dot(
            att[h * group : (h + 1) * group, :], wv[h], preferred_element_type=F32
        ).astype(BF)
        for g in range(NY):
            out[g, h * TOK : (h + 1) * TOK, :] = mixed[g * TOK : (g + 1) * TOK, :]


def merge_kernel(p_ref, out, flat):
    stats = [p_ref[s, QROWS:, :].astype(F32) for s in range(NY)]
    peaks = [v[0:4] + v[4:8] + v[8:12] for v in stats]
    totals = [v[12:16] + v[16:20] + v[20:24] for v in stats]
    peak = functools.reduce(jnp.maximum, peaks)
    weights = [t * jnp.exp(p - peak) for t, p in zip(totals, peaks)]
    total = functools.reduce(jnp.add, weights)
    mixed = sum(
        p_ref[s, 0:QROWS, :].astype(F32) * row_to_column(weights[s] / total) for s in range(NY)
    )
    for h in range(HEADS):
        flat[pl.ds(h, TOK, stride=HEADS), :] = mixed[h * TOK : (h + 1) * TOK, :]
    out[...] = flat[...].reshape(TOK, HEADS, 128).astype(BF)


def mirrored():
    ring = NH * NZ

    def index(r):
        return r % NZ * NH + r // NZ

    pairs = []
    for r in range(ring):
        first, offset = r // NR * NR, r % NR
        partner = first - 1 - offset if offset < NR // 2 else first + 2 * NR - 1 - offset
        pairs.append((index(r), index(partner % ring)))
    return pairs


def on_device(
    hidden, latent_proj, norm_gain, queries, key_absorb, value_absorb, pool_blocks, hit_block
):
    y, zl, c, x = (lax.axis_index(a) for a in ("y", ("zq", "zr"), "c", "x"))
    owner = hit_block // POOL_HERE
    ids = jnp.concatenate(
        [
            jnp.stack([y, x]),
            owner // (NZ * NC),
            (owner // NC) % NZ,
            jnp.stack([zl, c]),
            hit_block % POOL_HERE,
            owner % NC,
        ]
    ).astype(jnp.int32)
    first = HITS * BLOCK + ((y * NZ + zl) * NC + c) * TOK
    positions = (first + jnp.arange(TOK)).astype(F32)
    half = ROPE // 2
    inverse = 10000.0 ** (-jnp.arange(half, dtype=F32) / half)
    angle = positions[:, None] * inverse[None, :]
    cosine, sine = jnp.cos(angle), jnp.sin(angle)
    cosine = jnp.concatenate([cosine, cosine], axis=1)
    sine = jnp.concatenate([-sine, sine], axis=1)

    sent = pl.pallas_call(
        prepare_kernel,
        out_shape=jax.ShapeDtypeStruct((NY, PAYR, LANES), BF),
        in_specs=[SMEM] + [VMEM] * 3 + [pl.BlockSpec(memory_space=pltpu.HBM)],
        out_specs=VMEM,
        scratch_shapes=[
            pltpu.VMEM((QROWS, 128), F32),
            pltpu.VMEM((QROWS, 128), F32),
            pltpu.VMEM((HITS, WIDTH, BLOCK), BF),
            pltpu.VMEM((HITS * BLOCK, WIDTH), F32),
            pltpu.SemaphoreType.DMA((HITS,)),
        ],
        compiler_params=params(),
        name="prepare",
    )(hit_block, queries, cosine, sine, jnp.swapaxes(pool_blocks, 1, 2))
    received = lax.all_to_all(sent, "y", 0, 0)

    partial = pl.pallas_call(
        project_kernel,
        out_shape=jax.ShapeDtypeStruct((NX, RAWR, LANES), F32),
        in_specs=[VMEM] * 2,
        out_specs=VMEM,
        compiler_params=params(PROJ_MIB),
        name="project",
    )(hidden, latent_proj.T)
    mine = jnp.sum(lax.all_to_all(partial, "x", 0, 0), axis=0)
    other = lax.ppermute(mine, "zh", [(0, 1), (1, 0)])
    def whole(shape):
        return pl.BlockSpec(shape, lambda i: (0,) * len(shape))

    packed = pl.pallas_call(
        norm_kernel,
        grid=(1,),
        out_shape=jax.ShapeDtypeStruct((NR, ZROWS, LANES), BF),
        in_specs=[
            SMEM,
            whole((RAWR, LANES)),
            whole((RAWR, LANES)),
            whole((1, RANK)),
            whole((TOK, ROPE)),
            whole((TOK, ROPE)),
            whole((NY, PAY, LANES)),
        ],
        out_specs=whole((NR, ZROWS, LANES)),
        compiler_params=params(),
        name="norm",
    )(ids, mine, other, norm_gain[None, :], cosine, sine, received)
    quad = lax.all_to_all(packed, "zr", 0, 0)
    half = pl.pallas_call(
        half_kernel,
        out_shape=jax.ShapeDtypeStruct((HROWS, LANES), BF),
        in_specs=[SMEM, VMEM],
        out_specs=VMEM,
        compiler_params=params(),
        name="half",
    )(ids, quad)
    other_half = lax.ppermute(half, ("zq", "zr", "zh"), mirrored())
    packed = pl.pallas_call(
        pack_kernel,
        out_shape=jax.ShapeDtypeStruct((NX, CHUNK, LANES), BF),
        in_specs=[SMEM] + [VMEM] * 2,
        out_specs=VMEM,
        compiler_params=params(),
        name="pack",
    )(ids, half, other_half)
    along_x = lax.all_to_all(packed, "x", 0, 0)
    from_core = lax.ppermute(along_x, "c", [(0, 1), (1, 0)])
    qfull = pl.pallas_call(
        absorb_kernel,
        out_shape=jax.ShapeDtypeStruct((NY * QROWS, WIDTH), BF),
        in_specs=[VMEM] * 2,
        out_specs=VMEM,
        compiler_params=params(16),
        name="absorb",
    )(received, key_absorb)
    out = pl.pallas_call(
        attend_kernel,
        out_shape=jax.ShapeDtypeStruct((NY, OUTR, 128), BF),
        in_specs=[SMEM] + [VMEM] * 4,
        out_specs=VMEM,
        scratch_shapes=[
            pltpu.VMEM((KEYS, WIDTH), BF),
            pltpu.VMEM((NY * QROWS, RANK), BF),
        ],
        compiler_params=params(ATT_MIB),
        name="attend",
    )(ids, qfull, along_x, from_core, value_absorb)
    back = lax.all_to_all(out, "y", 0, 0)
    return pl.pallas_call(
        merge_kernel,
        out_shape=jax.ShapeDtypeStruct((TOK, HEADS, 128), BF),
        in_specs=[VMEM],
        out_specs=VMEM,
        scratch_shapes=[pltpu.VMEM((QROWS, 128), F32)],
        compiler_params=params(),
        name="merge",
    )(back)


def solution(mesh):
    fine = Mesh(mesh.devices.reshape(NY, NZ // NR, NR, NC, NH, NX), CTX + HEAD)
    placed = (
        P(CTX, HEAD),
        P(HEAD, None),
        P(),
        P(CTX, HEAD, None),
        P(HEAD, None, None),
        P(HEAD, None, None),
        P(CTX, None, None),
        P(),
    )
    return jax.shard_map(
        on_device, mesh=fine, in_specs=placed, out_specs=P(CTX, HEAD, None), check_vma=False
    )
```

```python
import functools
import math

import jax
import jax.numpy as jnp
from jax import lax
from jax.experimental import pallas as pl
from jax.experimental.pallas import tpu as pltpu
from jax.sharding import Mesh, PartitionSpec as P

EPS = 1e-06
NEG = -1e30
BF = jnp.bfloat16
F32 = jnp.float32

NY, NZ, NC, NH, NX = 4, 8, 2, 2, 4
NR = NZ // 2
CTX = ("y", "zq", "zr", "c")
HEAD = ("zh", "x")

TOK = 64
RANK = 512
WIDTH = 576
NOPE = 128
ROPE = 64
QW = 192
HEADS = 8
BLOCK = 128
POOL_HERE = 4
HITS = 2
XROWS = TOK // NX
PREV = 8
PIECE = HITS * PREV
QROWS = TOK * HEADS
LANES = 128
ATT_MIB = 28
PROJ_MIB = 62
BANDS = RANK // LANES
PAY = (BANDS + 1) * PIECE
PAYQ = PAY + QROWS
PAYR = PAYQ + QROWS // 2
RAWR = BANDS * XROWS + XROWS // 2
ZBAND = XROWS + PIECE
ZROWS = BANDS * ZBAND + 16
HALF = NR * XROWS
HBAND = HALF + PIECE
HROPE = BANDS * HBAND
HPRE = HROPE + HALF // 2
HROWS = HPRE + PIECE
SPAN = NZ * XROWS
XBAND = SPAN + PIECE
XROPE = BANDS * XBAND
XPRE = XROPE + SPAN // 2
CHUNK = XPRE + PIECE
NEW = NC * NX * NZ * XROWS
PRE = NX * PIECE
KEYS = NEW + PRE
STAT = 32
OUTR = QROWS + STAT
ROWS = 512

VMEM = pl.BlockSpec(memory_space=pltpu.VMEM)
SMEM = pl.BlockSpec(memory_space=pltpu.SMEM)


def params(mib=32):
    return pltpu.CompilerParams(vmem_limit_bytes=mib * 2**20)


def swap_halves(v):
    half = v.shape[-1] // 2
    return jnp.concatenate([v[:, half:], v[:, :half]], axis=1)


def prepare_kernel(hit, q_ref, cos_ref, sin_ref, pool_ref, out, qn, qr, found, pre, sem):
    x = lax.axis_index("x")
    copies = [
        pltpu.make_async_copy(pool_ref.at[lax.rem(hit[b], POOL_HERE)], found.at[b], sem.at[b])
        for b in range(HITS)
    ]
    for copy in copies:
        copy.start()
    flat = q_ref[...].astype(F32).reshape(QROWS, QW)
    qn[...] = flat[:, :NOPE]
    qr[:, :ROPE] = flat[:, NOPE:]
    cosine = cos_ref[...]
    sine = sin_ref[...]
    ropes = []
    for h in range(HEADS):
        rope = qr[pl.ds(h, TOK, stride=HEADS), :][:, :ROPE]
        ropes.append(rope * cosine + swap_halves(rope) * sine)
        rows = qn[pl.ds(h, TOK, stride=HEADS), :].astype(BF)
        for g in range(NY):
            out[g, PAY + h * TOK : PAY + (h + 1) * TOK, :] = rows
    for h in range(HEADS // 2):
        rows = jnp.concatenate([ropes[h], ropes[h + HEADS // 2]], axis=1).astype(BF)
        for g in range(NY):
            out[g, PAYQ + h * TOK : PAYQ + (h + 1) * TOK, :] = rows
    for b in range(HITS):
        copies[b].wait()
        pre[b * BLOCK : (b + 1) * BLOCK, :] = found[b].astype(F32).T
    quarter = BLOCK // NX
    blocks = [
        pre[pl.ds(pl.multiple_of(b * BLOCK + x * quarter, quarter), quarter), :]
        for b in range(HITS)
    ]
    for g in range(NY):
        piece = jnp.concatenate([v[g * PREV : (g + 1) * PREV] for v in blocks], axis=0)
        piece = jnp.concatenate([piece, piece[:, RANK:]], axis=1).astype(BF)
        for s in range(BANDS + 1):
            out[g, s * PIECE : (s + 1) * PIECE, :] = piece[:, s * LANES : (s + 1) * LANES]


def project_kernel(hidden, proj, out):
    partial = lax.dot_general(
        hidden[...], proj[...], (((1,), (1,)), ((), ())), preferred_element_type=F32
    )
    for k in range(NX):
        rows = partial[k * XROWS : (k + 1) * XROWS]
        for s in range(BANDS):
            out[k, s * XROWS : (s + 1) * XROWS, :] = rows[:, s * LANES : (s + 1) * LANES]
        rope = rows[:, RANK:]
        half = XROWS // 2
        out[k, BANDS * XROWS :, :] = jnp.concatenate([rope[:half], rope[half:]], axis=1)


def norm_kernel(ids, s_ref, r_ref, gain_ref, cos_ref, sin_ref, p_ref, out):
    x = ids[1]
    raw = s_ref[...] + r_ref[...]
    latent = jnp.concatenate([raw[s * XROWS : (s + 1) * XROWS] for s in range(BANDS)], axis=1)
    rope = raw[BANDS * XROWS :]
    rope = jnp.concatenate([rope[:, :ROPE], rope[:, ROPE:]], axis=0)
    mean = jnp.mean(latent * latent, axis=1, keepdims=True)
    scaled = (latent * lax.rsqrt(mean + EPS) * gain_ref[...]).astype(BF)
    start = pl.multiple_of(x * XROWS, XROWS)
    cosine = cos_ref[pl.ds(start, XROWS), :]
    sine = sin_ref[pl.ds(start, XROWS), :]
    rope = rope * cosine + swap_halves(rope) * sine
    row = lax.broadcasted_iota(jnp.int32, (PIECE, LANES), 0)
    bands = []
    for s in range(BANDS + 1):
        first = p_ref[ids[2], s * PIECE : (s + 1) * PIECE, :].astype(F32)
        second = p_ref[ids[3], s * PIECE : (s + 1) * PIECE, :].astype(F32)
        bands.append(jnp.where(row < PREV, first, second))
    ropes = jnp.concatenate([rope, bands[BANDS][:, :ROPE]], axis=1).astype(BF)
    for k in range(NR):
        for s in range(BANDS):
            n = s * ZBAND
            out[k, n : n + XROWS, :] = scaled[:, s * LANES : (s + 1) * LANES]
            out[k, n + XROWS : n + ZBAND, :] = bands[s].astype(BF)
        out[k, BANDS * ZBAND :, :] = ropes


def pick(first, second):
    row = lax.broadcasted_iota(jnp.int32, (PIECE, LANES), 0)
    return jnp.where(row < PREV, first.astype(F32), second.astype(F32))


def half_kernel(ids, z_ref, out):
    first, second = lax.rem(ids[4], NR), lax.rem(ids[5], NR)
    n = BANDS * ZBAND
    for s in range(BANDS):
        for k in range(NR):
            m = s * HBAND + k * XROWS
            out[m : m + XROWS, :] = z_ref[k, s * ZBAND : s * ZBAND + XROWS, :]
        m = s * ZBAND + XROWS
        band = pick(z_ref[first, m : m + PIECE, :], z_ref[second, m : m + PIECE, :])
        out[s * HBAND + HALF : (s + 1) * HBAND, :] = band.astype(BF)
    for k in range(NR // 2):
        m = HROPE + k * XROWS
        out[m : m + XROWS, :] = jnp.concatenate(
            [z_ref[i, n : n + XROWS, :][:, :ROPE] for i in (k, k + NR // 2)], axis=1
        )
    band = pick(z_ref[first, n : n + PIECE, :], z_ref[second, n : n + PIECE, :])
    out[HPRE:, :] = jnp.concatenate([band[:, ROPE:], band[:, ROPE:]], axis=1).astype(BF)


def pack_kernel(ids, own, other, out):
    quad = lax.div(ids[6], NR)
    mine = [lax.div(ids[4 + b], NR) == quad for b in range(HITS)]

    def piece(m):
        a = own[m : m + PIECE, :].astype(F32)
        b = other[m : m + PIECE, :].astype(F32)
        return pick(*[jnp.where(here, a, b) for here in mine]).astype(BF)

    bands = [piece(s * HBAND + HALF) for s in range(BANDS)]
    last = piece(HPRE)
    for k in range(NX):
        for i, ref in enumerate((own, other)):
            for s in range(BANDS):
                n = s * XBAND + i * HALF
                out[k, n : n + HALF, :] = ref[s * HBAND : s * HBAND + HALF, :]
            n = XROPE + i * (HALF // 2)
            out[k, n : n + HALF // 2, :] = ref[HROPE:HPRE, :]
        for s in range(BANDS):
            out[k, s * XBAND + SPAN : (s + 1) * XBAND, :] = bands[s]
        out[k, XPRE:, :] = last


def three(v):
    high = v.astype(BF).astype(F32)
    mid = (v - high).astype(BF).astype(F32)
    low = v - high - mid
    return [high, mid, low]


def absorb_kernel(q_ref, wk, qfull):
    group = NY * TOK
    for h in range(HEADS):
        k = PAY + h * TOK
        rows = jnp.concatenate([q_ref[g, k : k + TOK, :] for g in range(NY)], axis=0)
        k = PAYQ + h % (HEADS // 2) * TOK
        ropes = jnp.concatenate([q_ref[g, k : k + TOK, :] for g in range(NY)], axis=0)
        ropes = ropes[:, :ROPE] if h < HEADS // 2 else ropes[:, ROPE:]
        absorbed = jnp.dot(rows, wk[h], preferred_element_type=F32).astype(BF)
        full = jnp.concatenate([absorbed, ropes], axis=1)
        qfull[h * group : (h + 1) * group, :] = full


def attend_kernel(ids, qfull, here, there, wv, out, keys, att):
    y = ids[0]
    zl = ids[6]
    c = ids[7]
    scale = 1.0 / math.sqrt(QW)
    for i, ref in enumerate((here, there)):
        for j in range(NX):
            n = (i * NX + j) * SPAN
            for s in range(BANDS):
                keys[n : n + SPAN, s * LANES : (s + 1) * LANES] = ref[
                    j, s * XBAND : s * XBAND + SPAN, :
                ]
            ropes = ref[j, XROPE:XPRE, :]
            for k in range(4):
                m = k // 2 * (HALF // 2)
                part = ropes[m : m + HALF // 2]
                part = part[:, :ROPE] if k % 2 == 0 else part[:, ROPE:]
                keys[n + k * (HALF // 2) : n + (k + 1) * (HALF // 2), RANK:] = part
    for j in range(NX):
        n = NEW + j * PIECE
        for s in range(BANDS + 1):
            first = s * XBAND + SPAN if s < BANDS else XPRE
            mine = here[j, first : first + PIECE, :].astype(F32)
            other = there[j, first : first + PIECE, :].astype(F32)
            band = pick(
                jnp.where(ids[10] == c, mine, other), jnp.where(ids[11] == c, mine, other)
            ).astype(BF)
            if s < BANDS:
                keys[n : n + PIECE, s * LANES : (s + 1) * LANES] = band
            else:
                keys[n : n + PIECE, RANK:] = band[:, :ROPE]
    group = NY * TOK
    col = lax.broadcasted_iota(jnp.int32, (1, KEYS), 1)
    slot = lax.rem(lax.div(col, XROWS), NZ)
    quad = lax.div(zl, NR)
    zz = jnp.where(slot < NR, quad, 1 - quad) * NR + lax.rem(slot, NR)
    xx = lax.rem(lax.div(col, XROWS * NZ), NX)
    cc = lax.div(col, XROWS * NZ * NX)
    cc = jnp.where(cc == 0, c, 1 - c)
    token = zz * (NC * TOK) + cc * TOK + xx * XROWS + lax.rem(col, XROWS) + y * (NZ * NC * TOK)
    token = jnp.where(col < NEW, token, -1)
    row = lax.rem(lax.broadcasted_iota(jnp.int32, (ROWS, 1), 0), group)
    mine = lax.div(row, TOK) * (NZ * NC * TOK) + (zl * NC + c) * TOK
    visible = token <= mine + lax.rem(row, TOK)

    def score(i):
        return lax.dot_general(
            qfull[i * ROWS : (i + 1) * ROWS, :],
            keys[...],
            (((1,), (1,)), ((), ())),
            preferred_element_type=F32,
        )

    blocks = NY * QROWS // ROWS
    peaks, totals = [], []
    scores = score(0)
    for i in range(blocks):
        later = score(i + 1) if i + 1 < blocks else None
        scores = jnp.where(visible, scores, NEG)
        peak = jnp.max(scores, axis=1, keepdims=True)
        weights = jnp.exp2((scores - peak) * (scale * math.log2(math.e)))
        total = jnp.sum(weights, axis=1, keepdims=True)
        accum = jnp.dot(weights.astype(BF), keys[:, :RANK], preferred_element_type=F32)
        att[i * ROWS : (i + 1) * ROWS, :] = (accum / total).astype(BF)
        peaks.append(peak * scale)
        totals.append(total)
        scores = later
    stats = three(jnp.concatenate(peaks, axis=0)) + three(jnp.concatenate(totals, axis=0))
    blank = jnp.zeros((NY * QROWS, 8 - len(stats)), F32)
    table = jnp.concatenate(stats + [blank], axis=1)
    for g in range(NY):
        first = [table[h * group + g * TOK : h * group + (g + 1) * TOK] for h in range(HEADS)]
        turned = jnp.concatenate(first, axis=0).T
        parts = [
            turned[k : k + 1, i * LANES : (i + 1) * LANES]
            for k in range(len(stats))
            for i in range(QROWS // LANES)
        ]
        parts.append(jnp.zeros((STAT - 4 * len(stats), 128), F32))
        out[g, QROWS:, :] = jnp.concatenate(parts, axis=0).astype(BF)
    for h in range(HEADS):
        mixed = jnp.dot(
            att[h * group : (h + 1) * group, :], wv[h], preferred_element_type=F32
        ).astype(BF)
        for g in range(NY):
            out[g, h * TOK : (h + 1) * TOK, :] = mixed[g * TOK : (g + 1) * TOK, :]


def merge_kernel(p_ref, out, flat):
    stats = [p_ref[s, QROWS:, :].astype(F32) for s in range(NY)]
    peaks = [v[0:4] + v[4:8] + v[8:12] for v in stats]
    totals = [v[12:16] + v[16:20] + v[20:24] for v in stats]
    peak = functools.reduce(jnp.maximum, peaks)
    weights = [t * jnp.exp(p - peak) for t, p in zip(totals, peaks)]
    total = functools.reduce(jnp.add, weights)
    share = jnp.concatenate([w / total for w in weights], axis=0).T
    bands = QROWS // LANES
    columns = [
        jnp.concatenate([share[:, s * bands + i :][:, :1] for i in range(bands)], axis=0)
        for s in range(NY)
    ]
    mixed = sum(p_ref[s, 0:QROWS, :].astype(F32) * columns[s] for s in range(NY))
    for h in range(HEADS):
        flat[pl.ds(h, TOK, stride=HEADS), :] = mixed[h * TOK : (h + 1) * TOK, :]
    out[...] = flat[...].reshape(TOK, HEADS, 128).astype(BF)


def mirrored():
    ring = NH * NZ

    def index(r):
        return r % NZ * NH + r // NZ

    pairs = []
    for r in range(ring):
        first, offset = r // NR * NR, r % NR
        partner = first - 1 - offset if offset < NR // 2 else first + 2 * NR - 1 - offset
        pairs.append((index(r), index(partner % ring)))
    return pairs


def on_device(
    hidden, latent_proj, norm_gain, queries, key_absorb, value_absorb, pool_blocks, hit_block
):
    y, zl, c, x = (lax.axis_index(a) for a in ("y", ("zq", "zr"), "c", "x"))
    owner = hit_block // POOL_HERE
    ids = jnp.concatenate(
        [
            jnp.stack([y, x]),
            owner // (NZ * NC),
            (owner // NC) % NZ,
            jnp.stack([zl, c]),
            hit_block % POOL_HERE,
            owner % NC,
        ]
    ).astype(jnp.int32)
    first = HITS * BLOCK + ((y * NZ + zl) * NC + c) * TOK
    positions = (first + jnp.arange(TOK)).astype(F32)
    half = ROPE // 2
    inverse = 10000.0 ** (-jnp.arange(half, dtype=F32) / half)
    angle = positions[:, None] * inverse[None, :]
    cosine, sine = jnp.cos(angle), jnp.sin(angle)
    cosine = jnp.concatenate([cosine, cosine], axis=1)
    sine = jnp.concatenate([-sine, sine], axis=1)

    sent = pl.pallas_call(
        prepare_kernel,
        out_shape=jax.ShapeDtypeStruct((NY, PAYR, LANES), BF),
        in_specs=[SMEM] + [VMEM] * 3 + [pl.BlockSpec(memory_space=pltpu.HBM)],
        out_specs=VMEM,
        scratch_shapes=[
            pltpu.VMEM((QROWS, 128), F32),
            pltpu.VMEM((QROWS, 128), F32),
            pltpu.VMEM((HITS, WIDTH, BLOCK), BF),
            pltpu.VMEM((HITS * BLOCK, WIDTH), F32),
            pltpu.SemaphoreType.DMA((HITS,)),
        ],
        compiler_params=params(),
        name="prepare",
    )(hit_block, queries, cosine, sine, jnp.swapaxes(pool_blocks, 1, 2))
    received = lax.all_to_all(sent, "y", 0, 0)

    partial = pl.pallas_call(
        project_kernel,
        out_shape=jax.ShapeDtypeStruct((NX, RAWR, LANES), F32),
        in_specs=[VMEM] * 2,
        out_specs=VMEM,
        compiler_params=params(PROJ_MIB),
        name="project",
    )(hidden, latent_proj.T)
    mine = jnp.sum(lax.all_to_all(partial, "x", 0, 0), axis=0)
    other = lax.ppermute(mine, "zh", [(0, 1), (1, 0)])
    def whole(shape):
        return pl.BlockSpec(shape, lambda i: (0,) * len(shape))

    packed = pl.pallas_call(
        norm_kernel,
        grid=(1,),
        out_shape=jax.ShapeDtypeStruct((NR, ZROWS, LANES), BF),
        in_specs=[
            SMEM,
            whole((RAWR, LANES)),
            whole((RAWR, LANES)),
            whole((1, RANK)),
            whole((TOK, ROPE)),
            whole((TOK, ROPE)),
            whole((NY, PAY, LANES)),
        ],
        out_specs=whole((NR, ZROWS, LANES)),
        compiler_params=params(),
        name="norm",
    )(ids, mine, other, norm_gain[None, :], cosine, sine, received)
    quad = lax.all_to_all(packed, "zr", 0, 0)
    half = pl.pallas_call(
        half_kernel,
        out_shape=jax.ShapeDtypeStruct((HROWS, LANES), BF),
        in_specs=[SMEM, VMEM],
        out_specs=VMEM,
        compiler_params=params(),
        name="half",
    )(ids, quad)
    other_half = lax.ppermute(half, ("zq", "zr", "zh"), mirrored())
    packed = pl.pallas_call(
        pack_kernel,
        out_shape=jax.ShapeDtypeStruct((NX, CHUNK, LANES), BF),
        in_specs=[SMEM] + [VMEM] * 2,
        out_specs=VMEM,
        compiler_params=params(),
        name="pack",
    )(ids, half, other_half)
    along_x = lax.all_to_all(packed, "x", 0, 0)
    from_core = lax.ppermute(along_x, "c", [(0, 1), (1, 0)])
    qfull = pl.pallas_call(
        absorb_kernel,
        out_shape=jax.ShapeDtypeStruct((NY * QROWS, WIDTH), BF),
        in_specs=[VMEM] * 2,
        out_specs=VMEM,
        compiler_params=params(16),
        name="absorb",
    )(received, key_absorb)
    out = pl.pallas_call(
        attend_kernel,
        out_shape=jax.ShapeDtypeStruct((NY, OUTR, 128), BF),
        in_specs=[SMEM] + [VMEM] * 4,
        out_specs=VMEM,
        scratch_shapes=[
            pltpu.VMEM((KEYS, WIDTH), BF),
            pltpu.VMEM((NY * QROWS, RANK), BF),
        ],
        compiler_params=params(ATT_MIB),
        name="attend",
    )(ids, qfull, along_x, from_core, value_absorb)
    back = lax.all_to_all(out, "y", 0, 0)
    return pl.pallas_call(
        merge_kernel,
        out_shape=jax.ShapeDtypeStruct((TOK, HEADS, 128), BF),
        in_specs=[VMEM],
        out_specs=VMEM,
        scratch_shapes=[pltpu.VMEM((QROWS, 128), F32)],
        compiler_params=params(),
        name="merge",
    )(back)


def solution(mesh):
    fine = Mesh(mesh.devices.reshape(NY, NZ // NR, NR, NC, NH, NX), CTX + HEAD)
    placed = (
        P(CTX, HEAD),
        P(HEAD, None),
        P(),
        P(CTX, HEAD, None),
        P(HEAD, None, None),
        P(HEAD, None, None),
        P(CTX, None, None),
        P(),
    )
    return jax.shard_map(
        on_device, mesh=fine, in_specs=placed, out_specs=P(CTX, HEAD, None), check_vma=False
    )
```
